256 devices in a mesh: seq: 32 (over x, y, core), head: 8 (over z).
Axes of the slice: x: 4, y: 4, z: 8, core: 2. Of those that a mesh axis runs over, the one named last changes fastest.
Arguments:
- hidden_rows: bfloat16 [4, 64, 8192], P(None, None, 'seq'), may hold values from -6 to 6
- norm_gain: bfloat16 [8192], P('seq'), may hold values from 0.099609375 to 1.8984375
- w_query: bfloat16 [8192, 8192], P('seq', 'head'), may hold values from -0.0625 to 0.0625
- key_up: bfloat16 [160, 1024], P(None, 'head'), may hold values from -0.5 to 0.5
- key_factors: bfloat16 [64, 160, 16384], P(None, None, 'seq'), may hold values from -150 to 150
- values: bfloat16 [64, 16384, 1024], P(None, 'seq', 'head'), may hold values from -6 to 6
- w_out: bfloat16 [8192, 8192], P('head', 'seq'), may hold values from -0.125 to 0.125
- lengths: int32 [64], replicated, may hold values from 2048 to 16384, as said below
- key_positions: int32 [64, 16384], P(None, 'seq'), may hold values from 0 to 32766, as said below
- query_start: int32 [64], replicated, may hold values from 2048 to 32767, as said below
Outputs:
- attended: bfloat16 [4, 64, 8192], P(None, None, 'seq')
The draws below stay inside these ranges and needn't reach their ends.
Inputs may be any that keep to these rules, and one draw needn't show every extreme that they name: `lengths`: slots at or past a request's length hold no token; one request has length 16384 and one has length 2048. `key_positions`: along the slots of a request the positions start at 0 and rise by 1 or 2 per slot. query_start: one more than the position of the request's last live slot; step t sits at query_start + t.
All inputs are finite; a program needn't handle non-finite values.
Results may differ from the reference program's by a relative error of at most 0.013.
The reference program's roundings to bfloat16 on the way count: a program that leaves them out, or rounds other values in their place, can miss the bound.
Values may be sent and summed in bfloat16 or wider, within the bound.
A program may use at most 192 MiB of HBM per device.

```python
import jax
import jax.numpy as jnp
from jax import lax

D = 8192
HQ = 64
KVH = 8
HD = 128
R = 160
STEPS = 4
REQ = 64
GROUP = 8
CTX = 16384


def cache_layout(key):
    key_length = jax.random.fold_in(key, 101)
    key_full = jax.random.fold_in(key, 102)
    key_short = jax.random.fold_in(key, 103)
    key_spacing = jax.random.fold_in(key, 104)
    lengths = jax.random.randint(key_length, (REQ,), CTX // 8, CTX + 1)
    full_request = jax.random.randint(key_full, (), 0, REQ)
    short_request = (full_request + 1 + jax.random.randint(key_short, (), 0, REQ - 1)) % REQ
    request_ids = jnp.arange(REQ, dtype=jnp.int32)
    lengths = jnp.where(request_ids == full_request, CTX, jnp.where(request_ids == short_request, CTX // 8, lengths))
    spacing = jax.random.randint(key_spacing, (REQ, CTX), 1, 3)
    spacing = jnp.where((request_ids == full_request)[:, None], 2, spacing)
    positions = jnp.cumsum(spacing, axis=1) - spacing[:, :1]
    last_position = jnp.take_along_axis(positions, (lengths - 1)[:, None], axis=1)[:, 0]
    return (lengths.astype(jnp.int32), positions.astype(jnp.int32), (last_position + 1).astype(jnp.int32))


def draw_lengths(key, part):
    return cache_layout(key)[0]


def draw_key_positions(key, part):
    return cache_layout(key)[1]


def draw_query_start(key, part):
    return cache_layout(key)[2]


def draw_key_factors(key, part):
    key = jax.random.fold_in(key, 11)
    subkeys = jax.random.split(key, 1)
    factors = 2.5 * jax.random.truncated_normal(subkeys[0], -6.0, 6.0, (REQ, R, CTX), jnp.float32)
    return jnp.clip(factors, -150.0, 150.0).astype(jnp.bfloat16)


def levels(stream_key, shape, pieces, low, top_value):
    factor_of = 1.0
    for dim, blocks in pieces:
        heights = jax.random.uniform(jax.random.fold_in(jax.random.fold_in(stream_key, 6), dim), (blocks,), jnp.float32, low / len(pieces), top_value / len(pieces))
        factor_of = factor_of * jnp.repeat(jnp.exp(heights), shape[dim] // blocks).reshape((-1,) + (1,) * (len(shape) - 1 - dim))
    return factor_of


def gaussian(rng, dims, scale, bound, pieces=(), kind=jnp.bfloat16):
    array = scale * jax.random.normal(rng, dims, jnp.float32)
    if pieces:
        array = array * levels(rng, dims, pieces, -0.22, 0.18)
    return jnp.clip(array, -bound, bound).astype(kind)


def setup_inputs(seed: int = 0) -> dict:
    seeds = jax.random.split(jax.random.key(seed), 11)
    hidden_rows = gaussian(seeds[0], (STEPS, REQ, D), 1.0, 6.0, ((2, 32),))
    norm_gain = jnp.clip(1.0 + 0.18 * jax.random.normal(seeds[1], (D,), jnp.float32), 0.099609375, 1.8984375).astype(jnp.bfloat16)
    w_query = gaussian(seeds[2], (D, HQ * HD), D ** -0.5, 0.0625, ((0, 32), (1, 8)))
    key_up = gaussian(seeds[3], (R, KVH * HD), R ** -0.5, 0.5, ((1, 8),))
    key_factors = draw_key_factors(jax.random.fold_in(seeds[10], 71), 0)
    values = gaussian(seeds[5], (REQ, CTX, KVH * HD), 1.0, 6.0, ((1, 32), (2, 8)))
    w_out = gaussian(seeds[6], (HQ * HD, D), (HQ * HD // 4) ** -0.5, 0.125, ((0, 8), (1, 32)))
    lengths = draw_lengths(jax.random.fold_in(seeds[10], 71), 0)
    key_positions = draw_key_positions(jax.random.fold_in(seeds[10], 71), 0)
    query_start = draw_query_start(jax.random.fold_in(seeds[10], 71), 0)
    return dict(hidden_rows=hidden_rows, norm_gain=norm_gain, w_query=w_query, key_up=key_up, key_factors=key_factors, values=values, w_out=w_out, lengths=lengths, key_positions=key_positions, query_start=query_start)


ROPE_BASE = 500000.0
NORM_EPSILON = 1e-05

def rope_table(positions):
    half_width = HD // 2
    freq_index = jnp.arange(half_width, dtype=jnp.float32)
    inverse = jnp.power(jnp.float32(ROPE_BASE), -2.0 * freq_index / HD)
    angles = positions.astype(jnp.float32)[..., None] * inverse
    return (jnp.cos(angles), jnp.sin(angles))

def rotate(field, cosine_table, sine_table):
    half_width = HD // 2
    lower_half = field[..., :half_width]
    upper_half = field[..., half_width:]
    return jnp.concatenate([lower_half * cosine_table - upper_half * sine_table, upper_half * cosine_table + lower_half * sine_table], axis=-1)

def reference(hidden_rows, norm_gain, w_query, key_up, key_factors, values, w_out, lengths, key_positions, query_start):
    widened = hidden_rows.astype(jnp.float32)
    mean_square = lax.optimization_barrier(jnp.sum(widened * widened, axis=-1)) / D
    normed = (widened * norm_gain.astype(jnp.float32)).astype(jnp.bfloat16)
    projected = jnp.dot(normed.reshape(STEPS * REQ, D), w_query, preferred_element_type=jnp.float32)
    projected = projected.reshape(STEPS, REQ, HQ, HD) * lax.rsqrt(mean_square + NORM_EPSILON)[:, :, None, None]
    step_pos = query_start[None, :] + jnp.arange(STEPS, dtype=jnp.int32)[:, None]
    cosine_table, sine_table = rope_table(step_pos)
    queries = (rotate(projected, cosine_table[:, :, None, :], sine_table[:, :, None, :]) * HD ** (-0.5)).astype(jnp.bfloat16)
    queries = jnp.transpose(queries.reshape(STEPS, REQ, KVH, GROUP, HD), (1, 0, 2, 3, 4))
    up_wide = key_up.astype(jnp.float32)

    def one_request(items):
        query_rows, factors, cached, length, positions = items
        unrotated = jnp.dot(factors.astype(jnp.float32).T, up_wide).reshape(CTX, KVH, HD)
        key_cos, key_sin = rope_table(positions)
        rebuilt = rotate(unrotated, key_cos[:, None, :], key_sin[:, None, :]).astype(jnp.bfloat16)
        scores = jnp.einsum('thgd,chd->thgc', query_rows.astype(jnp.float32), rebuilt.astype(jnp.float32))
        is_live = jnp.arange(CTX, dtype=jnp.int32) < length
        scores = jnp.where(is_live, scores, -jnp.inf)
        row_top = lax.optimization_barrier(jnp.max(scores, axis=-1, keepdims=True))
        exponent = jnp.where(is_live, jnp.exp(scores - row_top), 0.0)
        row_total = lax.optimization_barrier(jnp.sum(exponent, axis=-1))
        weights = lax.optimization_barrier(exponent.astype(jnp.bfloat16)).astype(jnp.float32)
        weighted = jnp.einsum('thgc,chd->thgd', weights, cached.reshape(CTX, KVH, HD).astype(jnp.float32))
        return (weighted / row_total[..., None]).astype(jnp.bfloat16)
    mixed = lax.map(one_request, (queries, key_factors, values, lengths, key_positions))
    mixed = jnp.transpose(mixed, (1, 0, 2, 3, 4)).reshape(STEPS * REQ, HQ * HD)
    output = jnp.dot(mixed, w_out, preferred_element_type=jnp.float32)
    return output.reshape(STEPS, REQ, D).astype(jnp.bfloat16)
```

```python
import functools

import jax
import jax.numpy as jnp
import numpy as np
from jax import lax
from jax.experimental import pallas as pl
from jax.experimental.pallas import tpu as pltpu
from jax.sharding import PartitionSpec as P

HD = 128
HALF = 64
GROUP = 8
ROPE_BASE = 500000.0
NORM_EPSILON = 1e-05
DEAD = -1e30
MESH = pl.DeviceIdType.MESH
BF16 = jnp.bfloat16
F32 = jnp.float32
UNROLL = 4
KEYS_BEFORE_QUERIES = 0.5


def turn_tables():
    turns = ROPE_BASE ** (-2.0 * np.arange(HALF) / HD) / (2 * np.pi)
    mantissa, power = np.frexp(turns)
    head = np.ldexp(np.round(mantissa * 512) / 512, power)
    tail = turns - head
    rows = np.zeros((8, HD))
    rows[0], rows[1] = np.tile(head, 2), np.tile(tail, 2)
    columns = [np.broadcast_to(v[:, None], (HALF, HD)) for v in (head, tail)]
    return np.concatenate([*columns, rows]).astype(np.float32)


def chebyshev(function, terms):
    fit = np.polynomial.chebyshev.Chebyshev.interpolate(function, terms - 1, domain=[0, 0.25])
    return fit.convert(kind=np.polynomial.Polynomial).coef


COSINE = chebyshev(lambda z: np.cos(2 * np.pi * np.sqrt(z)), 7)
SINE = chebyshev(lambda z: 2 * np.pi * np.sinc(2 * np.sqrt(z)), 6)


def horner(coefficients, z):
    total = z * float(coefficients[-1]) + float(coefficients[-2])
    for c in coefficients[-3::-1]:
        total = total * z + float(c)
    return total


def cos_sin(position, head, tail):
    coarse, fine = position * head, position * tail
    part = (coarse - jnp.round(coarse + fine)) + fine
    square = part * part
    return horner(COSINE, square), part * horner(SINE, square)


def kernel(
    n, m, steps, requests, width,
    hid_hbm, gain_hbm, wq_hbm, ku_hbm, fac_hbm, val_hbm, wo_hbm, len_ref, pos_hbm, start_ref, tab_hbm,
    out_ref,
    hid, gain, wq, ku, fac, val, wo, pos, tab, keys,
    part_f32, a_out, a_in, row_f32, q_all, o_out, s_out, o_in, s_in, d_all, e_f32, e_out, e_in, y_all,
    load_sem, fac_sem, val_sem, send_sem, recv_sem,
):
    me, hd = lax.axis_index("seq"), lax.axis_index("head")
    slots = fac.shape[2]
    rows = steps * requests
    pair = requests // n
    per_step = requests // 8

    def seq_peer(d):
        return lax.rem(me + d, n)

    def head_peer(d):
        return lax.rem(hd + d, m)

    def send(src, dst, phase, peer, other):
        return pltpu.make_async_remote_copy(
            src_ref=src, dst_ref=dst, send_sem=send_sem.at[phase], recv_sem=recv_sem.at[phase],
            device_id=(peer, other), device_id_type=MESH,
        )

    def all_seq(phase, src_of, dst_of):
        def one(d, _):
            peer = seq_peer(d)
            send(src_of(peer), dst_of(d), phase, peer, hd).start()
            return 0

        lax.fori_loop(1, n, one, 0)

    def all_head(phase, src_of, dst_of):
        def one(d, _):
            peer = head_peer(d)
            send(src_of(peer), dst_of(d), phase, me, peer).start()
            return 0

        lax.fori_loop(1, m, one, 0)

    def wait_recv(phase, ref):
        send(ref, ref, phase, seq_peer(1), hd).wait_recv()

    def wait_send(phase, ref):
        send(ref, ref, phase, seq_peer(1), hd).wait_send()

    first = [(hid_hbm, hid), (gain_hbm, gain), (wq_hbm, wq), (tab_hbm, tab), (ku_hbm, ku), (pos_hbm, pos), (wo_hbm, wo)]
    loads = [pltpu.make_async_copy(src, dst, load_sem.at[i]) for i, (src, dst) in enumerate(first)]
    for copy in loads[:3]:
        copy.start()

    barrier = pltpu.get_barrier_semaphore()

    def greet_seq(d, _):
        pl.semaphore_signal(barrier, inc=1, device_id=(seq_peer(d), hd), device_id_type=MESH)
        return 0

    def greet_head(d, _):
        pl.semaphore_signal(barrier, inc=1, device_id=(me, head_peer(d)), device_id_type=MESH)
        return 0

    lax.fori_loop(1, n, greet_seq, 0)
    lax.fori_loop(1, m, greet_head, 0)
    for copy in loads[3:]:
        copy.start()

    def fac_load(i):
        block = pl.ds(i * UNROLL, UNROLL)
        return pltpu.make_async_copy(fac_hbm.at[block], fac.at[block], fac_sem.at[i])

    def val_load(o):
        block = pl.ds(o * pair, pair)
        return pltpu.make_async_copy(val_hbm.at[block], val.at[block], val_sem.at[o])

    def start_fac(i, _):
        fac_load(i).start()
        return 0

    def start_val(o, _):
        val_load(o).start()
        return 0

    lax.fori_loop(0, requests // UNROLL, start_fac, 0)

    for copy in loads[:3]:
        copy.wait()
    widened = hid[...].astype(F32)
    squares = jnp.sum(widened * widened, axis=-1, keepdims=True)
    normed = (widened * gain[...].astype(F32)).astype(BF16)
    for g in range(GROUP):
        term = jnp.dot(normed, wq[:, g * HD : (g + 1) * HD], preferred_element_type=F32)
        part_f32[:, g * 8 : (g + 1) * 8, :] = term.reshape(n, 8, HD)
    squares = jnp.broadcast_to(squares, (rows, HD)).reshape(n, 8, HD)
    square_head = squares.astype(BF16).astype(F32)
    a_out[:, 64:80, :] = jnp.concatenate([square_head, squares - square_head], axis=1).astype(BF16)
    a_out[:, 0:64, :] = part_f32[...].astype(BF16)

    pl.semaphore_wait(barrier, n + m - 2)
    all_seq(0, lambda peer: a_out.at[peer], lambda d: a_in.at[n - 1 - d])
    lax.fori_loop(0, n, start_val, 0)

    for copy in loads[3:]:
        copy.wait()
    up_rows = ku[...].T

    def build_keys(i, _):
        fac_load(i).wait()
        for u in range(UNROLL):
            b = i * UNROLL + u
            raw = jnp.dot(up_rows, fac[b], preferred_element_type=F32)
            where = pos[pl.ds(b, 1), :].astype(F32)
            for block in range(slots // HD):
                cut = slice(block * HD, (block + 1) * HD)
                cosine, sine = cos_sin(where[:, cut], tab[0:HALF, :], tab[HALF : 2 * HALF, :])
                lower, upper = raw[0:HALF, cut], raw[HALF:HD, cut]
                keys[b, 0:HALF, cut] = (lower * cosine - upper * sine).astype(BF16)
                keys[b, HALF:HD, cut] = (upper * cosine + lower * sine).astype(BF16)
        return 0

    key_steps = requests // UNROLL
    early = int(key_steps * KEYS_BEFORE_QUERIES)
    lax.fori_loop(0, early, build_keys, 0)

    wait_recv(0, a_in)

    def add_term(k, total):
        return total + a_in[k].astype(F32)

    own = jnp.concatenate([part_f32[me], a_out[me, 64:80, :].astype(F32)], axis=0)
    total = lax.fori_loop(0, n - 1, add_term, own)
    mean_square = (total[64:72] + total[72:80]) * (1.0 / width)
    projected = total[0:64].reshape(GROUP, 8, HD) * lax.rsqrt(mean_square + NORM_EPSILON)[None]
    step = me // per_step
    first_request = (me - step * per_step) * 8
    sublane = lax.broadcasted_iota(jnp.int32, (8, HD), 0)
    lane = lax.broadcasted_iota(jnp.int32, (8, HD), 1)
    where = jnp.zeros((8, HD), jnp.int32)
    for r in range(8):
        where = jnp.where(sublane == r, start_ref[first_request + r] + step, where)
    cosine, sine = cos_sin(where.astype(F32), tab[HD : HD + 1, :], tab[HD + 1 : HD + 2, :])
    sine = jnp.where(lane < HALF, -sine, sine)
    flat = projected.reshape(64, HD)
    turned = pltpu.roll(flat, HALF, 1).reshape(GROUP, 8, HD)
    queries = (projected * cosine[None] + turned * sine[None]) * HD ** (-0.5)
    row_f32[...] = queries.reshape(64, HD)
    by_request = [row_f32[pl.ds(r, 8, stride=8), :] for r in range(8)]
    q_all[me] = jnp.concatenate(by_request, axis=0).astype(BF16)
    all_seq(1, lambda peer: q_all.at[me], lambda d: q_all.at[me])

    lax.fori_loop(early, key_steps, build_keys, 0)
    wait_recv(1, q_all.at[pl.ds(0, n - 1)])

    slot = lax.broadcasted_iota(jnp.int32, (1, slots), 1) + me * slots
    row32 = lax.broadcasted_iota(jnp.int32, (steps * GROUP, HD), 0)
    lane32 = lax.broadcasted_iota(jnp.int32, (steps * GROUP, HD), 1)

    def attend(o):
        val_load(o).wait()
        b0 = o * pair
        tile = b0 // 8
        inside = pl.multiple_of((b0 - tile * 8) * 8, 16)
        both = [q_all[t * per_step + tile, pl.ds(inside, 8 * pair), :].astype(F32) for t in range(steps)]
        stats = jnp.zeros((1, HD), F32)
        mixes = []
        for j in range(pair):
            q = jnp.concatenate([x[8 * j : 8 * j + 8] for x in both], axis=0).astype(BF16)
            scores = jnp.dot(q, keys[b0 + j], preferred_element_type=F32)
            live = slot < len_ref[b0 + j]
            scores = jnp.where(live, scores, DEAD)
            top = jnp.max(scores, axis=1, keepdims=True)
            exponent = jnp.where(live, jnp.exp(scores - top), 0.0)
            total = jnp.sum(exponent, axis=1, keepdims=True)
            mixes.append(jnp.dot(exponent.astype(BF16), val[b0 + j], preferred_element_type=F32))
            spot = row32 + steps * GROUP * j
            spread = jnp.where(lane32 == spot, top, jnp.where(lane32 == spot + HALF, total, 0.0))
            stats = stats + jnp.sum(spread, axis=0, keepdims=True)
        return jnp.concatenate(mixes, axis=0).astype(BF16), stats

    def two_owners(k, _):
        for u in range(2):
            o = lax.rem(me + 1 + 2 * k + u, n)
            mix, stats = attend(o)
            o_out[o], s_out[o] = mix, stats

            @pl.when(o != me)
            def _():
                send(o_out.at[o], o_in.at[me], 2, o, hd).start()
                send(s_out.at[o], s_in.at[me], 3, o, hd).start()

        return 0

    lax.fori_loop(0, n // 2, two_owners, 0)
    o_in[me], s_in[me] = o_out[me], s_out[me]
    wait_recv(3, s_in.at[pl.ds(0, n - 1)])
    stats = s_in[...].reshape(n, HD)
    is_top = lax.broadcasted_iota(jnp.int32, (n, HD), 1) < HALF
    scale = jnp.where(is_top, jnp.exp(jnp.minimum(stats - jnp.max(stats, axis=0, keepdims=True), 0.0)), 0.0)
    row_total = jnp.sum(scale * pltpu.roll(stats, HALF, 1), axis=0, keepdims=True)
    share = jnp.where(is_top, scale / jnp.where(is_top[0:1], row_total, 1.0), 0.0).T
    wait_recv(2, o_in.at[pl.ds(0, n - 1)])
    mixed = jnp.zeros((64, HD), F32)
    for k in range(n):
        mixed = mixed + share[0:64, k : k + 1] * o_in[k].astype(F32)
    row_f32[...] = mixed
    by_head = [row_f32[pl.ds(g, 8, stride=8), :] for g in range(GROUP)]
    d_all[me] = jnp.concatenate(by_head, axis=0).astype(BF16)
    all_seq(4, lambda peer: d_all.at[me], lambda d: d_all.at[me])
    wait_recv(4, d_all.at[pl.ds(0, n - 1)])

    wide = d_all[...].astype(F32)
    wide = [wide[:, g * 8 : (g + 1) * 8, :].reshape(rows, HD) for g in range(GROUP)]
    wide = jnp.concatenate(wide, axis=1).astype(BF16)
    term = jnp.dot(wide, wo[...], preferred_element_type=F32).reshape(e_f32.shape)
    e_f32[...] = term
    e_out[...] = term.astype(BF16)
    all_head(5, lambda peer: e_out.at[peer], lambda d: e_in.at[m - 1 - d])
    wait_recv(5, e_in)
    total = e_f32[hd]
    for k in range(m - 1):
        total = total + e_in[k].astype(F32)
    y_all[hd] = total.astype(BF16)
    all_head(6, lambda peer: y_all.at[hd], lambda d: y_all.at[hd])
    wait_recv(6, y_all.at[pl.ds(0, m - 1)])
    out_ref[...] = y_all[...]

    wait_send(0, a_in)
    wait_send(1, q_all.at[pl.ds(0, n - 1)])
    wait_send(2, o_in.at[pl.ds(0, n - 1)])
    wait_send(3, s_in.at[pl.ds(0, n - 1)])
    wait_send(4, d_all.at[pl.ds(0, n - 1)])
    wait_send(5, e_in)
    wait_send(6, y_all.at[pl.ds(0, m - 1)])


def solution(mesh):
    n, m = mesh.shape["seq"], mesh.shape["head"]

    def per_device(hidden_rows, norm_gain, w_query, key_up, key_factors, values, w_out, lengths, key_positions, query_start):
        steps, requests, features = hidden_rows.shape
        rows = steps * requests
        slots, rank = key_factors.shape[2], key_factors.shape[1]
        columns = w_out.shape[1]
        table = turn_tables()
        vmem, sem = pltpu.VMEM, pltpu.SemaphoreType.DMA
        hbm, smem = pl.BlockSpec(memory_space=pl.ANY), pl.BlockSpec(memory_space=pltpu.SMEM)
        y = pl.pallas_call(
            functools.partial(kernel, n, m, steps, requests, features * n),
            out_shape=jax.ShapeDtypeStruct((m, rows // m, columns), BF16),
            in_specs=[hbm, hbm, hbm, hbm, hbm, hbm, hbm, smem, hbm, smem, hbm],
            out_specs=pl.BlockSpec(memory_space=vmem),
            scratch_shapes=[
                vmem((rows, features), BF16),
                vmem((1, features), BF16),
                vmem(w_query.shape, BF16),
                vmem(key_up.shape, BF16),
                vmem((requests, rank, slots), BF16),
                vmem((requests, slots, HD), BF16),
                vmem(w_out.shape, BF16),
                vmem((requests, slots), jnp.int32),
                vmem(table.shape, F32),
                vmem((requests, HD, slots), BF16),
                vmem((n, 64, HD), F32),
                vmem((n, 80, HD), BF16),
                vmem((n - 1, 80, HD), BF16),
                vmem((64, HD), F32),
                vmem((n, 64, HD), BF16),
                vmem((n, 64, HD), BF16),
                vmem((n, 1, HD), F32),
                vmem((n, 64, HD), BF16),
                vmem((n, 1, HD), F32),
                vmem((n, 64, HD), BF16),
                vmem((m, rows // m, columns), F32),
                vmem((m, rows // m, columns), BF16),
                vmem((m - 1, rows // m, columns), BF16),
                vmem((m, rows // m, columns), BF16),
                sem((7,)),
                sem((requests // UNROLL,)),
                sem((n,)),
                sem((7,)),
                sem((7,)),
            ],
            compiler_params=pltpu.CompilerParams(
                collective_id=0, has_side_effects=True, vmem_limit_bytes=56 * 2**20
            ),
            name="decode",
        )(
            hidden_rows.reshape(rows, features), norm_gain.reshape(1, features), w_query, key_up, key_factors,
            values, w_out, lengths, key_positions, query_start, jnp.asarray(table),
        )
        return y.reshape(requests, steps, columns).transpose(1, 0, 2)

    return jax.shard_map(
        per_device,
        mesh=mesh,
        in_specs=(
            P(None, None, "seq"),
            P("seq"),
            P("seq", "head"),
            P(None, "head"),
            P(None, None, "seq"),
            P(None, "seq", "head"),
            P("head", "seq"),
            P(),
            P(None, "seq"),
            P(),
        ),
        out_specs=P(None, None, "seq"),
        check_vma=False,
    )
```

```python
import functools
import math

import jax
import jax.numpy as jnp
import numpy as np
from jax import lax
from jax.experimental import pallas as pl
from jax.experimental.pallas import tpu as pltpu
from jax.sharding import PartitionSpec as P

HD = 128
HALF = 64
GROUP = 8
ROPE_BASE = 500000.0
NORM_EPSILON = 1e-05
DEAD = -1e30
MESH = pl.DeviceIdType.MESH
BF16 = jnp.bfloat16
F32 = jnp.float32
UNROLL = 4
KEY_CUTS = (0.125, 0.5, 0.9375)


def turn_tables():
    turns = ROPE_BASE ** (-2.0 * np.arange(HALF) / HD) / (2 * np.pi)
    mantissa, power = np.frexp(turns)
    head = np.ldexp(np.round(mantissa * 512) / 512, power)
    tail = turns - head
    rows = np.zeros((8, HD))
    rows[0], rows[1] = np.tile(head, 2), np.tile(tail, 2)
    columns = [np.broadcast_to(v[:, None], (HALF, HD)) for v in (head, tail)]
    return np.concatenate([*columns, rows]).astype(np.float32)


def chebyshev(function, terms):
    fit = np.polynomial.chebyshev.Chebyshev.interpolate(function, terms - 1, domain=[0, 0.25])
    return fit.convert(kind=np.polynomial.Polynomial).coef


COSINE = chebyshev(lambda z: np.cos(2 * np.pi * np.sqrt(z)), 7)
SINE = chebyshev(lambda z: 2 * np.pi * np.sinc(2 * np.sqrt(z)), 6)


def horner(coefficients, z):
    total = z * float(coefficients[-1]) + float(coefficients[-2])
    for c in coefficients[-3::-1]:
        total = total * z + float(c)
    return total


def cos_sin(position, head, tail):
    coarse, fine = position * head, position * tail
    part = (coarse - jnp.round(coarse + fine)) + fine
    square = part * part
    return horner(COSINE, square), part * horner(SINE, square)


def far_first(k, size):
    return lax.rem(2 + k + (k * (k - 1)) // 2, 4) if size == 4 else lax.rem(k + 1, size)


def kernel(
    n, m, steps, requests, width,
    hid_hbm, gain_hbm, wq_hbm, ku_hbm, fac_hbm, val_hbm, wo_hbm, len_ref, pos_hbm, start_ref, tab_hbm,
    out_ref,
    hid, gain, wq, ku, fac, val, wo, pos, tab, keys,
    part, a_sib_out, a_sib_in, a_out, a_in, row_f32, q_all, o_out, s_out, o_in, s_in, d_all, e_f32, e_out, e_in, y_all,
    y_f32, y_rows, load_sem, fac_sem, val_sem, send_sem, recv_sem,
):
    me, hd = lax.axis_index("seq"), lax.axis_index("head")
    chip, core = me // 2, lax.rem(me, 2)
    other = 1 - core
    sibling = chip * 2 + other
    chips = n // 2
    side = math.isqrt(chips)
    slots = fac.shape[2]
    rows = steps * requests
    pair = requests // n
    per_step = requests // 8
    half_rows = rows // 2

    def chip_at(d):
        return lax.rem(chip + d, chips), chips - 1 - d

    def copy_to(src, dst, phase, peer, head):
        return pltpu.make_async_remote_copy(
            src_ref=src, dst_ref=dst, send_sem=send_sem.at[phase], recv_sem=recv_sem.at[phase],
            device_id=(peer, head), device_id_type=MESH,
        )

    def to_chips(phase, src_of, dst_of):
        def one(d, _):
            peer, place = chip_at(d)
            copy_to(src_of(peer), dst_of(place), phase, peer * 2 + core, hd).start()
            return 0

        lax.fori_loop(1, chips, one, 0)

    def wait_recv(phase, ref):
        copy_to(ref, ref, phase, sibling, hd).wait_recv()

    def wait_send(phase, ref):
        copy_to(ref, ref, phase, sibling, hd).wait_send()

    first = [(hid_hbm, hid), (gain_hbm, gain), (wq_hbm, wq), (tab_hbm, tab), (ku_hbm, ku), (pos_hbm, pos), (wo_hbm, wo)]
    loads = [pltpu.make_async_copy(src, dst, load_sem.at[i]) for i, (src, dst) in enumerate(first)]
    for copy in loads[:3]:
        copy.start()

    barrier = pltpu.get_barrier_semaphore()

    def greet_seq(d, _):
        pl.semaphore_signal(barrier, inc=1, device_id=(lax.rem(me + d, n), hd), device_id_type=MESH)
        return 0

    def greet_head(d, _):
        pl.semaphore_signal(barrier, inc=1, device_id=(me, lax.rem(hd + d, m)), device_id_type=MESH)
        return 0

    lax.fori_loop(1, n, greet_seq, 0)
    lax.fori_loop(1, m, greet_head, 0)
    for copy in loads[3:]:
        copy.start()

    def fac_load(i):
        block = pl.ds(i * UNROLL, UNROLL)
        return pltpu.make_async_copy(fac_hbm.at[block], fac.at[block], fac_sem.at[i])

    def val_load(o):
        block = pl.ds(o * pair, pair)
        return pltpu.make_async_copy(val_hbm.at[block], val.at[block], val_sem.at[o])

    def start_fac(i, _):
        fac_load(i).start()
        return 0

    def start_val(o, _):
        val_load(o).start()
        return 0

    key_steps = requests // UNROLL
    lax.fori_loop(0, key_steps, start_fac, 0)

    for copy in loads[:3]:
        copy.wait()
    widened = hid[...].astype(F32)
    squares = jnp.sum(widened * widened, axis=-1, keepdims=True)
    normed = (widened * gain[...].astype(F32).reshape(1, -1)).astype(BF16)
    for g in range(GROUP):
        term = jnp.dot(normed, wq[:, g * HD : (g + 1) * HD], preferred_element_type=F32)
        part[:, :, g * 8 : (g + 1) * 8, :] = term.reshape(chips, 2, 8, HD)
    part[:, :, 64:72, :] = jnp.broadcast_to(squares, (rows, HD)).reshape(chips, 2, 8, HD)

    def packed(block):
        square = block[:, 64:72]
        head = square.astype(BF16).astype(F32)
        return jnp.concatenate([block[:, 0:64], head, square - head], axis=1).astype(BF16)

    def unpacked(block):
        block = block.astype(F32)
        return jnp.concatenate([block[..., 0:64, :], block[..., 64:72, :] + block[..., 72:80, :]], axis=-2)

    a_sib_out[...] = packed(part[:, other])
    pl.semaphore_wait(barrier, n + m - 2)
    copy_to(a_sib_out, a_sib_in, 0, sibling, hd).start()
    lax.fori_loop(0, n, start_val, 0)

    for copy in loads[3:]:
        copy.wait()
    up_rows = ku[...].T

    def build_keys(i, _):
        fac_load(i).wait()
        for u in range(UNROLL):
            b = i * UNROLL + u
            raw = jnp.dot(up_rows, fac[b], preferred_element_type=F32)
            where = pos[pl.ds(b, 1), :].astype(F32)
            for block in range(slots // HD):
                cut = slice(block * HD, (block + 1) * HD)
                cosine, sine = cos_sin(where[:, cut], tab[0:HALF, :], tab[HALF : 2 * HALF, :])
                lower, upper = raw[0:HALF, cut], raw[HALF:HD, cut]
                keys[b, 0:HALF, cut] = (lower * cosine - upper * sine).astype(BF16)
                keys[b, HALF:HD, cut] = (upper * cosine + lower * sine).astype(BF16)
        return 0

    cuts = [round(key_steps * f) for f in KEY_CUTS]
    lax.fori_loop(0, cuts[0], build_keys, 0)
    wait_recv(0, a_sib_in)
    both_cores = part[:, core] + unpacked(a_sib_in[...])
    part[:, core] = both_cores
    a_out[...] = packed(both_cores)
    to_chips(1, lambda peer: a_out.at[peer], lambda place: a_in.at[place])
    lax.fori_loop(cuts[0], cuts[1], build_keys, 0)

    wait_recv(1, a_in)
    total = lax.fori_loop(0, chips - 1, lambda k, x: x + unpacked(a_in[k]), part[chip, core])
    mean_square = total[64:72] * (1.0 / width)
    projected = total[0:64].reshape(GROUP, 8, HD) * lax.rsqrt(mean_square + NORM_EPSILON)[None]
    step = me // per_step
    first_request = (me - step * per_step) * 8
    sublane = lax.broadcasted_iota(jnp.int32, (8, HD), 0)
    lane = lax.broadcasted_iota(jnp.int32, (8, HD), 1)
    where = jnp.zeros((8, HD), jnp.int32)
    for r in range(8):
        where = jnp.where(sublane == r, start_ref[first_request + r] + step, where)
    cosine, sine = cos_sin(where.astype(F32), tab[HD : HD + 1, :], tab[HD + 1 : HD + 2, :])
    sine = jnp.where(lane < HALF, -sine, sine)
    flat = projected.reshape(64, HD)
    turned = pltpu.roll(flat, HALF, 1).reshape(GROUP, 8, HD)
    queries = (projected * cosine[None] + turned * sine[None]) * HD ** (-0.5)
    row_f32[...] = queries.reshape(64, HD)
    by_request = [row_f32[pl.ds(r, 8, stride=8), :] for r in range(8)]
    q_all[core, chip] = jnp.concatenate(by_request, axis=0).astype(BF16)
    mine = q_all.at[core, chip]
    to_chips(2, lambda peer: mine, lambda place: mine)
    lax.fori_loop(cuts[1], cuts[2], build_keys, 0)
    wait_recv(2, q_all.at[0, pl.ds(0, chips - 1)])
    copy_to(q_all.at[core], q_all.at[core], 3, sibling, hd).start()
    lax.fori_loop(cuts[2], key_steps, build_keys, 0)
    wait_recv(3, q_all.at[0])

    slot = lax.broadcasted_iota(jnp.int32, (1, slots), 1) + me * slots
    row32 = lax.broadcasted_iota(jnp.int32, (steps * GROUP, HD), 0)
    lane32 = lax.broadcasted_iota(jnp.int32, (steps * GROUP, HD), 1)

    def attend(o):
        b0 = o * pair
        tile = b0 // 8
        inside = pl.multiple_of((b0 - tile * 8) * 8, 16)
        both = []
        for t in range(steps):
            from_rows = t * per_step + tile
            both.append(q_all[lax.rem(from_rows, 2), from_rows // 2, pl.ds(inside, 8 * pair), :].astype(F32))
        stats = jnp.zeros((1, HD), F32)
        mixes = []
        for j in range(pair):
            q = jnp.concatenate([x[8 * j : 8 * j + 8] for x in both], axis=0).astype(BF16)
            scores = jnp.dot(q, keys[b0 + j], preferred_element_type=F32)
            live = slot < len_ref[b0 + j]
            scores = jnp.where(live, scores, DEAD)
            top = jnp.max(scores, axis=1, keepdims=True)
            exponent = jnp.where(live, jnp.exp(scores - top), 0.0)
            total = jnp.sum(exponent, axis=1, keepdims=True)
            mixes.append(jnp.dot(exponent.astype(BF16), val[b0 + j], preferred_element_type=F32))
            spot = row32 + steps * GROUP * j
            spread = jnp.where(lane32 == spot, top, jnp.where(lane32 == spot + HALF, total, 0.0))
            stats = stats + jnp.sum(spread, axis=0, keepdims=True)
        return jnp.concatenate(mixes, axis=0).astype(BF16), stats

    x, y = chip // side, lax.rem(chip, side)

    def send_mix(o):
        copy_to(o_out.at[o], o_in.at[me], 4, o, hd).start()
        copy_to(s_out.at[o], s_in.at[me], 5, o, hd).start()

    def two_chips(i, _):
        owners = []
        for k in (2 * i, 2 * i + 1):
            over = lax.rem(x + far_first(k // side, side), side) * side
            over += lax.rem(y + far_first(lax.rem(k, side), side), side)
            owners += [over * 2 + other, over * 2 + core]
        for o in owners:
            val_load(o).wait()
        found = [attend(o) for o in owners]
        for o, (mix, stats) in zip(owners, found):
            o_out[o], s_out[o] = mix, stats
        for o in owners[:3]:
            send_mix(o)

        @pl.when(i < chips // 2 - 1)
        def _():
            send_mix(owners[3])

        return 0

    lax.fori_loop(0, chips // 2, two_chips, 0)
    o_in[me], s_in[me] = o_out[me], s_out[me]
    wait_recv(5, s_in.at[pl.ds(0, n - 1)])
    stats = s_in[...].reshape(n, HD)
    is_top = lax.broadcasted_iota(jnp.int32, (n, HD), 1) < HALF
    scale = jnp.where(is_top, jnp.exp(jnp.minimum(stats - jnp.max(stats, axis=0, keepdims=True), 0.0)), 0.0)
    row_total = jnp.sum(scale * pltpu.roll(stats, HALF, 1), axis=0, keepdims=True)
    share = jnp.where(is_top, scale / jnp.where(is_top[0:1], row_total, 1.0), 0.0).T
    wait_recv(4, o_in.at[pl.ds(0, n - 1)])
    mixed = jnp.zeros((64, HD), F32)
    for k in range(n):
        mixed = mixed + share[0:64, k : k + 1] * o_in[k].astype(F32)
    row_f32[...] = mixed
    by_head = [row_f32[pl.ds(g, 8, stride=8), :] for g in range(GROUP)]
    d_all[core, chip] = jnp.concatenate(by_head, axis=0).astype(BF16)
    own_rows = d_all.at[core, chip]
    to_chips(6, lambda peer: own_rows, lambda place: own_rows)
    wait_recv(6, d_all.at[0, pl.ds(0, chips - 1)])
    copy_to(d_all.at[core], d_all.at[core], 7, sibling, hd).start()

    pieces = m // 2

    def project(side_of):
        wide = d_all[side_of].astype(F32)
        wide = [wide[:, g * 8 : (g + 1) * 8, :].reshape(half_rows, HD) for g in range(GROUP)]
        wide = jnp.concatenate(wide, axis=1).astype(BF16)
        term = jnp.dot(wide, wo[...], preferred_element_type=F32).reshape(pieces, rows // m, wo.shape[1])
        e_f32[pl.ds(side_of * pieces, pieces)] = term
        e_out[pl.ds(side_of * pieces, pieces)] = term.astype(BF16)
        for j in range(pieces):
            to = side_of * pieces + lax.rem(hd + j, pieces)

            @pl.when(to != hd)
            def _():
                copy_to(e_out.at[to], e_in.at[lax.rem(hd - to - 1 + m, m)], 8, me, to).start()

    project(core)
    wait_recv(7, d_all.at[0])
    project(other)
    wait_recv(8, e_in)
    total = e_f32[hd]
    for k in range(m - 1):
        total = total + e_in[k].astype(F32)
    y_all[hd] = total.astype(BF16)

    def to_head(d, _):
        copy_to(y_all.at[hd], y_all.at[hd], 9, me, lax.rem(hd + d, m)).start()
        return 0

    lax.fori_loop(1, m, to_head, 0)
    wait_recv(9, y_all.at[pl.ds(0, m - 1)])
    gathered = y_all[...].astype(F32).reshape(rows, wo.shape[1])
    for strip in range(wo.shape[1] // HD):
        cut = slice(strip * HD, (strip + 1) * HD)
        y_f32[strip] = gathered[:, cut]
        for c in range(2):
            for j in range(pair):
                for t in range(steps):
                    block = y_f32[strip, pl.ds(c * half_rows + j * steps + t, chips, stride=8), :]
                    y_rows[strip, pl.ds(t * requests + c * pair + j, chips, stride=2 * pair), :] = block
        out_ref[:, cut] = y_rows[strip].astype(BF16)

    wait_send(0, a_sib_in)
    wait_send(1, a_in)
    wait_send(2, q_all.at[0, pl.ds(0, chips - 1)])
    wait_send(3, q_all.at[0])
    wait_send(4, o_in.at[pl.ds(0, n - 1)])
    wait_send(5, s_in.at[pl.ds(0, n - 1)])
    wait_send(6, d_all.at[0, pl.ds(0, chips - 1)])
    wait_send(7, d_all.at[0])
    wait_send(8, e_in)
    wait_send(9, y_all.at[pl.ds(0, m - 1)])


def solution(mesh):
    n, m = mesh.shape["seq"], mesh.shape["head"]

    def per_device(hidden_rows, norm_gain, w_query, key_up, key_factors, values, w_out, lengths, key_positions, query_start):
        steps, requests, features = hidden_rows.shape
        rows = steps * requests
        slots, rank = key_factors.shape[2], key_factors.shape[1]
        columns = w_out.shape[1]
        table = turn_tables()
        vmem, sem = pltpu.VMEM, pltpu.SemaphoreType.DMA
        hbm, smem = pl.BlockSpec(memory_space=pl.ANY), pl.BlockSpec(memory_space=pltpu.SMEM)
        y = pl.pallas_call(
            functools.partial(kernel, n, m, steps, requests, features * n),
            out_shape=jax.ShapeDtypeStruct((rows, columns), BF16),
            in_specs=[hbm, hbm, hbm, hbm, hbm, hbm, hbm, smem, hbm, smem, hbm],
            out_specs=pl.BlockSpec(memory_space=vmem),
            scratch_shapes=[
                vmem((rows, features), BF16),
                vmem((features,), BF16),
                vmem(w_query.shape, BF16),
                vmem(key_up.shape, BF16),
                vmem((requests, rank, slots), BF16),
                vmem((requests, slots, HD), BF16),
                vmem(w_out.shape, BF16),
                vmem((requests, slots), jnp.int32),
                vmem(table.shape, F32),
                vmem((requests, HD, slots), BF16),
                vmem((n // 2, 2, 72, HD), F32),
                vmem((n // 2, 80, HD), BF16),
                vmem((n // 2, 80, HD), BF16),
                vmem((n // 2, 80, HD), BF16),
                vmem((n // 2 - 1, 80, HD), BF16),
                vmem((64, HD), F32),
                vmem((2, n // 2, 64, HD), BF16),
                vmem((n, 64, HD), BF16),
                vmem((n, 1, HD), F32),
                vmem((n, 64, HD), BF16),
                vmem((n, 1, HD), F32),
                vmem((2, n // 2, 64, HD), BF16),
                vmem((m, rows // m, columns), F32),
                vmem((m, rows // m, columns), BF16),
                vmem((m - 1, rows // m, columns), BF16),
                vmem((m, rows // m, columns), BF16),
                vmem((columns // HD, rows, HD), F32),
                vmem((columns // HD, rows, HD), F32),
                sem((7,)),
                sem((requests // UNROLL,)),
                sem((n,)),
                sem((10,)),
                sem((10,)),
            ],
            compiler_params=pltpu.CompilerParams(
                collective_id=0, has_side_effects=True, vmem_limit_bytes=56 * 2**20
            ),
            name="decode",
        )(
            hidden_rows.reshape(rows, features), norm_gain, w_query, key_up, key_factors,
            values, w_out, lengths, key_positions, query_start, jnp.asarray(table),
        )
        return y.reshape(steps, requests, columns)

    return jax.shard_map(
        per_device,
        mesh=mesh,
        in_specs=(
            P(None, None, "seq"),
            P("seq"),
            P("seq", "head"),
            P(None, "head"),
            P(None, None, "seq"),
            P(None, "seq", "head"),
            P("head", "seq"),
            P(),
            P(None, "seq"),
            P(),
        ),
        out_specs=P(None, None, "seq"),
        check_vma=False,
    )
```

```python
import functools
import math

import jax
import jax.numpy as jnp
import numpy as np
from jax import lax
from jax.experimental import pallas as pl
from jax.experimental.pallas import tpu as pltpu
from jax.sharding import PartitionSpec as P

HD = 128
HALF = 64
GROUP = 8
ROPE_BASE = 500000.0
NORM_EPSILON = 1e-05
DEAD = -1e30
MESH = pl.DeviceIdType.MESH
BF16 = jnp.bfloat16
F32 = jnp.float32
UNROLL = 4
KEY_CUTS = (0.0625, 0.5, 0.9375)


def turn_tables():
    turns = ROPE_BASE ** (-2.0 * np.arange(HALF) / HD) / (2 * np.pi)
    mantissa, power = np.frexp(turns)
    head = np.ldexp(np.round(mantissa * 512) / 512, power)
    tail = turns - head
    rows = np.zeros((8, HD))
    rows[0], rows[1] = np.tile(head, 2), np.tile(tail, 2)
    columns = [np.broadcast_to(v[:, None], (HALF, HD)) for v in (head, tail)]
    return np.concatenate([*columns, rows]).astype(np.float32)


def chebyshev(function, terms):
    fit = np.polynomial.chebyshev.Chebyshev.interpolate(function, terms - 1, domain=[0, 0.25])
    return fit.convert(kind=np.polynomial.Polynomial).coef


COSINE = chebyshev(lambda z: np.cos(2 * np.pi * np.sqrt(z)), 7)
SINE = chebyshev(lambda z: 2 * np.pi * np.sinc(2 * np.sqrt(z)), 6)


def horner(coefficients, z):
    total = z * float(coefficients[-1]) + float(coefficients[-2])
    for c in coefficients[-3::-1]:
        total = total * z + float(c)
    return total


def cos_sin(position, head, tail):
    coarse, fine = position * head, position * tail
    part = (coarse - jnp.round(coarse + fine)) + fine
    square = part * part
    return horner(COSINE, square), part * horner(SINE, square)


def far_first(k, size):
    return lax.rem(2 + k + (k * (k - 1)) // 2, 4) if size == 4 else lax.rem(k + 1, size)


def kernel(
    n, m, steps, requests, width,
    hid_hbm, gain_hbm, wq_hbm, ku_hbm, fac_hbm, val_hbm, wo_hbm, len_hbm, pos_hbm, start_hbm, tab_hbm,
    out_ref,
    hid, gain, wq, ku, fac, val, wo, pos, tab, keys,
    part, a_sib_out, a_sib_in, a_out, a_in, row_f32, q_all, o_out, o_in, d_all, e_f32, e_out, e_in, y_all,
    y_f32, y_rows, len_ref, start_ref, load_sem, fac_sem, val_sem, send_sem, recv_sem,
):
    me, hd = lax.axis_index("seq"), lax.axis_index("head")
    chip, core = me // 2, lax.rem(me, 2)
    other = 1 - core
    sibling = chip * 2 + other
    chips = n // 2
    side = math.isqrt(chips)
    slots = fac.shape[2]
    rows = steps * requests
    pair = requests // n
    per_step = requests // 8
    half_rows = rows // 2

    x, y = chip // side, lax.rem(chip, side)

    def chip_at(k):
        over = lax.rem(x + far_first(k // side, side), side) * side
        return over + lax.rem(y + far_first(lax.rem(k, side), side), side)

    def head_at(k):
        away = (k + 1) // 2
        return lax.rem(hd + m + m // 2 + away - 2 * away * lax.rem(k, 2), m)

    def copy_to(src, dst, phase, peer, head):
        return pltpu.make_async_remote_copy(
            src_ref=src, dst_ref=dst, send_sem=send_sem.at[phase], recv_sem=recv_sem.at[phase],
            device_id=(peer, head), device_id_type=MESH,
        )

    def to_chips(phase, src_of, dst):
        def one(k, _):
            peer = chip_at(k)
            copy_to(src_of(peer), dst, phase, peer * 2 + core, hd).start()
            return 0

        lax.fori_loop(0, chips - 1, one, 0)

    def wait_recv(phase, ref):
        copy_to(ref, ref, phase, sibling, hd).wait_recv()

    def wait_send(phase, ref):
        copy_to(ref, ref, phase, sibling, hd).wait_send()

    first = [(hid_hbm, hid), (gain_hbm, gain), (wq_hbm, wq), (tab_hbm, tab), (ku_hbm, ku), (pos_hbm, pos), (wo_hbm, wo)]
    first += [(len_hbm, len_ref), (start_hbm, start_ref)]
    loads = [pltpu.make_async_copy(src, dst, load_sem.at[i]) for i, (src, dst) in enumerate(first)]
    for copy in loads[:3]:
        copy.start()

    barrier = pltpu.get_barrier_semaphore()

    def greet(peer, head):
        pl.semaphore_signal(barrier, inc=1, device_id=(peer, head), device_id_type=MESH)

    def greet_head(k, _):
        greet(me, head_at(k))
        return 0

    def greet_chip(k, _):
        peer = chip_at(k)
        greet(peer * 2, hd)
        greet(peer * 2 + 1, hd)
        return 0

    lax.fori_loop(0, m - 1, greet_head, 0)
    lax.fori_loop(0, chips - 1, greet_chip, 0)
    greet(sibling, hd)
    for copy in loads[3:]:
        copy.start()

    def fac_load(i):
        block = pl.ds(i * UNROLL, UNROLL)
        return pltpu.make_async_copy(fac_hbm.at[block], fac.at[block], fac_sem.at[i])

    def val_load(o):
        block = pl.ds(o * pair, pair)
        return pltpu.make_async_copy(val_hbm.at[block], val.at[block], val_sem.at[o])

    def start_fac(i, _):
        fac_load(i).start()
        return 0

    def start_val(o, _):
        val_load(o).start()
        return 0

    key_steps = requests // UNROLL
    lax.fori_loop(0, key_steps, start_fac, 0)

    for copy in loads[:3]:
        copy.wait()
    widened = hid[...].astype(F32)
    squares = jnp.sum(widened * widened, axis=-1, keepdims=True)
    normed = (widened * gain[...].astype(F32).reshape(1, -1)).astype(BF16)
    for g in range(GROUP):
        term = jnp.dot(normed, wq[:, g * HD : (g + 1) * HD], preferred_element_type=F32)
        part[:, :, g * 8 : (g + 1) * 8, :] = term.reshape(chips, 2, 8, HD)
    part[:, :, 64:72, :] = jnp.broadcast_to(squares, (rows, HD)).reshape(chips, 2, 8, HD)

    def packed(block):
        square = block[:, 64:72]
        head = square.astype(BF16).astype(F32)
        return jnp.concatenate([block[:, 0:64], head, square - head], axis=1).astype(BF16)

    def unpacked(block):
        block = block.astype(F32)
        return jnp.concatenate([block[..., 0:64, :], block[..., 64:72, :] + block[..., 72:80, :]], axis=-2)

    a_sib_out[...] = packed(part[:, other])
    pl.semaphore_wait(barrier, n + m - 2)
    copy_to(a_sib_out, a_sib_in, 0, sibling, hd).start()
    lax.fori_loop(0, n, start_val, 0)

    for copy in loads[3:]:
        copy.wait()
    up_rows = ku[...].T

    def build_keys(i, _):
        fac_load(i).wait()
        for u in range(UNROLL):
            b = i * UNROLL + u
            raw = jnp.dot(up_rows, fac[b], preferred_element_type=F32)
            where = pos[pl.ds(b, 1), :].astype(F32)
            for block in range(slots // HD):
                cut = slice(block * HD, (block + 1) * HD)
                cosine, sine = cos_sin(where[:, cut], tab[0:HALF, :], tab[HALF : 2 * HALF, :])
                lower, upper = raw[0:HALF, cut], raw[HALF:HD, cut]
                keys[b, 0:HALF, cut] = (lower * cosine - upper * sine).astype(BF16)
                keys[b, HALF:HD, cut] = (upper * cosine + lower * sine).astype(BF16)
        return 0

    cuts = [round(key_steps * f) for f in KEY_CUTS]
    lax.fori_loop(0, cuts[0], build_keys, 0)
    wait_recv(0, a_sib_in)
    both_cores = part[:, core] + unpacked(a_sib_in[...])
    part[:, core] = both_cores
    a_out[...] = packed(both_cores)
    to_chips(1, lambda peer: a_out.at[peer], a_in.at[chip])
    lax.fori_loop(cuts[0], cuts[1], build_keys, 0)

    wait_recv(1, a_in.at[pl.ds(0, chips - 1)])
    total = lax.fori_loop(1, chips, lambda k, t: t + unpacked(a_in[lax.rem(chip + k, chips)]), part[chip, core])
    mean_square = total[64:72] * (1.0 / width)
    projected = total[0:64].reshape(GROUP, 8, HD) * lax.rsqrt(mean_square + NORM_EPSILON)[None]
    step = me // per_step
    first_request = (me - step * per_step) * 8
    sublane = lax.broadcasted_iota(jnp.int32, (8, HD), 0)
    lane = lax.broadcasted_iota(jnp.int32, (8, HD), 1)
    where = jnp.zeros((8, HD), jnp.int32)
    for r in range(8):
        where = jnp.where(sublane == r, start_ref[first_request + r] + step, where)
    cosine, sine = cos_sin(where.astype(F32), tab[HD : HD + 1, :], tab[HD + 1 : HD + 2, :])
    sine = jnp.where(lane < HALF, -sine, sine)
    flat = projected.reshape(64, HD)
    turned = pltpu.roll(flat, HALF, 1).reshape(GROUP, 8, HD)
    queries = (projected * cosine[None] + turned * sine[None]) * HD ** (-0.5)
    row_f32[...] = queries.reshape(64, HD)
    by_request = [row_f32[pl.ds(r, 8, stride=8), :] for r in range(8)]
    q_all[core, chip] = jnp.concatenate(by_request, axis=0).astype(BF16)
    mine = q_all.at[core, chip]
    to_chips(2, lambda peer: mine, mine)
    lax.fori_loop(cuts[1], cuts[2], build_keys, 0)
    wait_recv(2, q_all.at[0, pl.ds(0, chips - 1)])
    copy_to(q_all.at[core], q_all.at[core], 3, sibling, hd).start()
    lax.fori_loop(cuts[2], key_steps, build_keys, 0)
    wait_recv(3, q_all.at[0])

    slot = lax.broadcasted_iota(jnp.int32, (1, slots), 1) + me * slots
    row32 = lax.broadcasted_iota(jnp.int32, (steps * GROUP, HD), 0)
    row16 = lax.broadcasted_iota(jnp.int32, (16, HD), 0)
    lane32 = lax.broadcasted_iota(jnp.int32, (steps * GROUP, HD), 1)

    def queries_of(o):
        tile = o * pair // 8
        inside = pl.multiple_of((o * pair - tile * 8) * 8, 16)
        both = []
        for t in range(steps):
            from_rows = t * per_step + tile
            both.append(q_all[lax.rem(from_rows, 2), from_rows // 2, pl.ds(inside, 8 * pair), :].astype(F32))
        return [jnp.concatenate([x[8 * j : 8 * j + 8] for x in both], axis=0).astype(BF16) for j in range(pair)]

    def attend(owners):
        queries = [q for o in owners for q in queries_of(o)]
        requests_here = [o * pair + j for o in owners for j in range(pair)]
        scores = [jnp.dot(q, keys[b], preferred_element_type=F32) for q, b in zip(queries, requests_here)]
        live = [slot < len_ref[b] for b in requests_here]
        scores = [jnp.where(ok, x, DEAD) for ok, x in zip(live, scores)]
        tops = [jnp.max(x, axis=1, keepdims=True) for x in scores]
        exponents = [jnp.where(ok, jnp.exp(x - top), 0.0) for ok, x, top in zip(live, scores, tops)]
        totals = [jnp.sum(x, axis=1, keepdims=True) for x in exponents]
        mixes = [jnp.dot(x.astype(BF16), val[b], preferred_element_type=F32) for x, b in zip(exponents, requests_here)]
        for i, o in enumerate(owners):
            stats = jnp.zeros((1, HD), F32)
            for j in range(pair):
                spot = row32 + steps * GROUP * j
                spread = jnp.where(lane32 == spot, tops[pair * i + j], jnp.where(lane32 == spot + HALF, totals[pair * i + j], 0.0))
                stats = stats + jnp.sum(spread, axis=0, keepdims=True)
            high = stats.astype(BF16).astype(F32)
            middle = (stats - high).astype(BF16).astype(F32)
            low = stats - high - middle
            tail = jnp.where(row16 == 0, high, jnp.where(row16 == 1, middle, jnp.where(row16 == 2, low, 0.0)))
            o_out[o] = jnp.concatenate([*mixes[pair * i : pair * (i + 1)], tail], axis=0).astype(BF16)

    def send_mix(o):
        copy_to(o_out.at[o], o_in.at[me], 4, o, hd).start()

    def two_chips(i, _):
        owners = []
        for k in (2 * i, 2 * i + 1):
            owners += [chip_at(k) * 2 + other, chip_at(k) * 2 + core]
        for o in owners:
            val_load(o).wait()
        attend(owners)
        for o in owners[:3]:
            send_mix(o)

        @pl.when(i < chips // 2 - 1)
        def _():
            send_mix(owners[3])

        return 0

    lax.fori_loop(0, chips // 2, two_chips, 0)
    o_in[me] = o_out[me]
    wait_recv(4, o_in.at[pl.ds(0, n - 1)])
    tails = o_in[:, 64:80, :].astype(F32)
    stats = jnp.sum(tails, axis=1)
    is_top = lax.broadcasted_iota(jnp.int32, (n, HD), 1) < HALF
    scale = jnp.where(is_top, jnp.exp(jnp.minimum(stats - jnp.max(stats, axis=0, keepdims=True), 0.0)), 0.0)
    row_total = jnp.sum(scale * pltpu.roll(stats, HALF, 1), axis=0, keepdims=True)
    share = jnp.where(is_top, scale / jnp.where(is_top[0:1], row_total, 1.0), 0.0).T
    mixed = jnp.zeros((64, HD), F32)
    for k in range(n):
        mixed = mixed + share[0:64, k : k + 1] * o_in[k, 0:64].astype(F32)
    row_f32[...] = mixed
    by_head = [row_f32[pl.ds(g, 8, stride=8), :] for g in range(GROUP)]
    d_all[core, chip] = jnp.concatenate(by_head, axis=0).astype(BF16)
    own_rows = d_all.at[core, chip]
    to_chips(6, lambda peer: own_rows, own_rows)
    wait_recv(6, d_all.at[0, pl.ds(0, chips - 1)])
    copy_to(d_all.at[core], d_all.at[core], 7, sibling, hd).start()

    pieces = m // 2

    def project(side_of):
        wide = d_all[side_of].astype(F32)
        wide = [wide[:, g * 8 : (g + 1) * 8, :].reshape(half_rows, HD) for g in range(GROUP)]
        wide = jnp.concatenate(wide, axis=1).astype(BF16)
        term = jnp.dot(wide, wo[...], preferred_element_type=F32).reshape(pieces, rows // m, wo.shape[1])
        e_f32[pl.ds(side_of * pieces, pieces)] = term
        e_out[pl.ds(side_of * pieces, pieces)] = term.astype(BF16)
        for j in range(pieces):
            to = side_of * pieces + lax.rem(hd + pieces // 2 + j, pieces)

            @pl.when(to != hd)
            def _():
                copy_to(e_out.at[to], e_in.at[lax.rem(hd - to - 1 + m, m)], 8, me, to).start()

    project(core)
    wait_recv(7, d_all.at[0])
    project(other)
    wait_recv(8, e_in)
    total = e_f32[hd]
    for k in range(m - 1):
        total = total + e_in[k].astype(F32)
    y_all[hd] = total.astype(BF16)

    def to_head(k, _):
        copy_to(y_all.at[hd], y_all.at[hd], 9, me, head_at(k)).start()
        return 0

    lax.fori_loop(0, m - 1, to_head, 0)
    wait_recv(9, y_all.at[pl.ds(0, m - 1)])
    gathered = y_all[...].astype(F32).reshape(rows, wo.shape[1])
    for strip in range(wo.shape[1] // HD):
        cut = slice(strip * HD, (strip + 1) * HD)
        y_f32[strip] = gathered[:, cut]
        for c in range(2):
            for j in range(pair):
                for t in range(steps):
                    block = y_f32[strip, pl.ds(c * half_rows + j * steps + t, chips, stride=8), :]
                    y_rows[strip, pl.ds(t * requests + c * pair + j, chips, stride=2 * pair), :] = block
        out_ref[:, cut] = y_rows[strip].astype(BF16)

    wait_send(0, a_sib_in)
    wait_send(1, a_in.at[pl.ds(0, chips - 1)])
    wait_send(2, q_all.at[0, pl.ds(0, chips - 1)])
    wait_send(3, q_all.at[0])
    wait_send(4, o_in.at[pl.ds(0, n - 1)])
    wait_send(6, d_all.at[0, pl.ds(0, chips - 1)])
    wait_send(7, d_all.at[0])
    wait_send(8, e_in)
    wait_send(9, y_all.at[pl.ds(0, m - 1)])


def solution(mesh):
    n, m = mesh.shape["seq"], mesh.shape["head"]

    def per_device(hidden_rows, norm_gain, w_query, key_up, key_factors, values, w_out, lengths, key_positions, query_start):
        steps, requests, features = hidden_rows.shape
        rows = steps * requests
        slots, rank = key_factors.shape[2], key_factors.shape[1]
        columns = w_out.shape[1]
        table = turn_tables()
        vmem, sem = pltpu.VMEM, pltpu.SemaphoreType.DMA
        hbm = pl.BlockSpec(memory_space=pl.ANY)
        y = pl.pallas_call(
            functools.partial(kernel, n, m, steps, requests, features * n),
            out_shape=pltpu.VMEM((rows, columns), BF16),
            in_specs=[hbm] * 11,
            out_specs=pl.BlockSpec(memory_space=vmem),
            scratch_shapes=[
                vmem((rows, features), BF16),
                vmem((features,), BF16),
                vmem(w_query.shape, BF16),
                vmem(key_up.shape, BF16),
                vmem((requests, rank, slots), BF16),
                vmem((requests, slots, HD), BF16),
                vmem(w_out.shape, BF16),
                vmem((requests, slots), jnp.int32),
                vmem(table.shape, F32),
                vmem((requests, HD, slots), BF16),
                vmem((n // 2, 2, 72, HD), F32),
                vmem((n // 2, 80, HD), BF16),
                vmem((n // 2, 80, HD), BF16),
                vmem((n // 2, 80, HD), BF16),
                vmem((n // 2, 80, HD), BF16),
                vmem((64, HD), F32),
                vmem((2, n // 2, 64, HD), BF16),
                vmem((n, 80, HD), BF16),
                vmem((n, 80, HD), BF16),
                vmem((2, n // 2, 64, HD), BF16),
                vmem((m, rows // m, columns), F32),
                vmem((m, rows // m, columns), BF16),
                vmem((m - 1, rows // m, columns), BF16),
                vmem((m, rows // m, columns), BF16),
                vmem((columns // HD, rows, HD), F32),
                vmem((columns // HD, rows, HD), F32),
                pltpu.SMEM((requests,), jnp.int32),
                pltpu.SMEM((requests,), jnp.int32),
                sem((9,)),
                sem((requests // UNROLL,)),
                sem((n,)),
                sem((10,)),
                sem((10,)),
            ],
            compiler_params=pltpu.CompilerParams(
                collective_id=0, has_side_effects=True, vmem_limit_bytes=56 * 2**20
            ),
            name="decode",
        )(
            hidden_rows.reshape(rows, features), norm_gain, w_query, key_up, key_factors,
            values, w_out, lengths, key_positions, query_start, jnp.asarray(table),
        )
        return y.reshape(steps, requests, columns)

    return jax.shard_map(
        per_device,
        mesh=mesh,
        in_specs=(
            P(None, None, "seq"),
            P("seq"),
            P("seq", "head"),
            P(None, "head"),
            P(None, None, "seq"),
            P(None, "seq", "head"),
            P("head", "seq"),
            P(),
            P(None, "seq"),
            P(),
        ),
        out_specs=P(None, None, "seq"),
        check_vma=False,
    )
```

```python
import functools
import math

import jax
import jax.numpy as jnp
import numpy as np
from jax import lax
from jax.experimental import pallas as pl
from jax.experimental.pallas import tpu as pltpu
from jax.sharding import PartitionSpec as P

HD = 128
HALF = 64
GROUP = 8
ROPE_BASE = 500000.0
NORM_EPSILON = 1e-05
DEAD = -1e30
MESH = pl.DeviceIdType.MESH
BF16 = jnp.bfloat16
F32 = jnp.float32
UNROLL = 4
KEY_CUTS = (0.125, 0.5, 0.875)
CHUNKS = 4


def turn_tables():
    turns = ROPE_BASE ** (-2.0 * np.arange(HALF) / HD) / (2 * np.pi)
    mantissa, power = np.frexp(turns)
    head = np.ldexp(np.round(mantissa * 512) / 512, power)
    tail = turns - head
    rows = np.zeros((8, HD))
    rows[0], rows[1] = np.tile(head, 2), np.tile(tail, 2)
    columns = [np.broadcast_to(v[:, None], (HALF, HD)) for v in (head, tail)]
    return np.concatenate([*columns, rows]).astype(np.float32)


def chebyshev(function, terms):
    fit = np.polynomial.chebyshev.Chebyshev.interpolate(function, terms - 1, domain=[0, 0.25])
    return fit.convert(kind=np.polynomial.Polynomial).coef


COSINE = chebyshev(lambda z: np.cos(2 * np.pi * np.sqrt(z)), 6)
SINE = chebyshev(lambda z: 2 * np.pi * np.sinc(2 * np.sqrt(z)), 5)


def horner(coefficients, z):
    total = z * float(coefficients[-1]) + float(coefficients[-2])
    for c in coefficients[-3::-1]:
        total = total * z + float(c)
    return total


def cos_sin(position, head, tail):
    coarse, fine = position * head, position * tail
    part = (coarse - jnp.round(coarse + fine)) + fine
    square = part * part
    return horner(COSINE, square), part * horner(SINE, square)


def far_first(k, size):
    return lax.rem(2 + k + (k * (k - 1)) // 2, 4) if size == 4 else lax.rem(k + 1, size)


def kernel(
    n, m, steps, requests, width,
    hid_hbm, gain_hbm, wq_hbm, ku_hbm, fac_hbm, val_hbm, wo_hbm, len_hbm, pos_hbm, start_hbm, tab_hbm,
    out_ref,
    hid, gain, wq, ku, fac, val, wo, pos, tab, keys,
    part, a_sib_out, a_sib_in, a_out, a_in, row_f32, q_all, o_sib_out, o_sib_in, o_out, o_in, d_all, e_f32, e_out, e_in, y_all,
    y_f32, y_rows, len_ref, start_ref, load_sem, fac_sem, val_sem, batch_sem, send_sem, recv_sem,
):
    me, hd = lax.axis_index("seq"), lax.axis_index("head")
    chip, core = me // 2, lax.rem(me, 2)
    other = 1 - core
    sibling = chip * 2 + other
    chips = n // 2
    side = math.isqrt(chips)
    slots = fac.shape[2]
    rows = steps * requests
    pair = requests // n
    per_step = requests // 8
    half_rows = rows // 2

    x, y = chip // side, lax.rem(chip, side)

    def chip_at(k):
        over = lax.rem(x + far_first(k // side, side), side) * side
        return over + lax.rem(y + far_first(lax.rem(k, side), side), side)

    def head_at(k):
        away = (k + 1) // 2
        return lax.rem(hd + m + m // 2 + away - 2 * away * lax.rem(k, 2), m)

    def copy_to(src, dst, phase, peer, head):
        return pltpu.make_async_remote_copy(
            src_ref=src, dst_ref=dst, send_sem=send_sem.at[phase], recv_sem=recv_sem.at[phase],
            device_id=(peer, head), device_id_type=MESH,
        )

    def to_chips(phase, src_of, dst):
        def one(k, _):
            peer = chip_at(k)
            copy_to(src_of(peer), dst, phase, peer * 2 + core, hd).start()
            return 0

        lax.fori_loop(0, chips - 1, one, 0)

    def wait_recv(phase, ref):
        copy_to(ref, ref, phase, sibling, hd).wait_recv()

    def wait_send(phase, ref):
        copy_to(ref, ref, phase, sibling, hd).wait_send()

    first = [(hid_hbm, hid), (gain_hbm, gain), (wq_hbm, wq), (tab_hbm, tab), (ku_hbm, ku), (pos_hbm, pos), (wo_hbm, wo)]
    first += [(len_hbm, len_ref), (start_hbm, start_ref)]
    loads = [pltpu.make_async_copy(src, dst, load_sem.at[i]) for i, (src, dst) in enumerate(first)]
    for copy in loads[:3]:
        copy.start()

    barrier = pltpu.get_barrier_semaphore()

    def greet(peer, head):
        pl.semaphore_signal(barrier, inc=1, device_id=(peer, head), device_id_type=MESH)

    def greet_head(k, _):
        greet(me, head_at(k))
        return 0

    def greet_chip(k, _):
        greet(chip_at(k) * 2 + core, hd)
        return 0

    lax.fori_loop(0, m - 1, greet_head, 0)
    lax.fori_loop(0, chips - 1, greet_chip, 0)
    greet(sibling, hd)
    for copy in loads[3:]:
        copy.start()

    def big_load(src, dst, sem, i):
        block = pl.ds(i * (requests // CHUNKS), requests // CHUNKS)
        return pltpu.make_async_copy(src.at[block], dst.at[block], sem.at[i])

    key_steps = requests // UNROLL
    chunk_steps = key_steps // CHUNKS
    for i in range(CHUNKS):
        big_load(fac_hbm, fac, fac_sem, i).start()

    for copy in loads[:3]:
        copy.wait()
    widened = hid[...].astype(F32)
    squares = jnp.sum(widened * widened, axis=-1, keepdims=True)
    normed = (widened * gain[...].astype(F32).reshape(1, -1)).astype(BF16)
    for g in range(GROUP):
        term = jnp.dot(normed, wq[:, g * HD : (g + 1) * HD], preferred_element_type=F32)
        part[:, :, g * 8 : (g + 1) * 8, :] = term.reshape(chips, 2, 8, HD)
    part[:, :, 64:72, :] = jnp.broadcast_to(squares, (rows, HD)).reshape(chips, 2, 8, HD)

    def packed(block):
        square = block[:, 64:72]
        head = square.astype(BF16).astype(F32)
        return jnp.concatenate([block[:, 0:64], head, square - head], axis=1).astype(BF16)

    def unpacked(block):
        block = block.astype(F32)
        return jnp.concatenate([block[..., 0:64, :], block[..., 64:72, :] + block[..., 72:80, :]], axis=-2)

    a_sib_out[...] = packed(part[:, other])
    pl.semaphore_wait(barrier, chips + m - 1)
    copy_to(a_sib_out, a_sib_in, 0, sibling, hd).start()
    for i in range(CHUNKS):
        big_load(val_hbm, val, val_sem, i).start()

    for copy in loads[3:]:
        copy.wait()
    up_rows = ku[...].T

    def build_keys(i, _):
        @pl.when(lax.rem(i, chunk_steps) == 0)
        def _():
            big_load(fac_hbm, fac, fac_sem, i // chunk_steps).wait()

        for u in range(UNROLL):
            b = i * UNROLL + u
            raw = jnp.dot(up_rows, fac[b], preferred_element_type=F32)
            where = pos[pl.ds(b, 1), :].astype(F32)
            for block in range(slots // HD):
                cut = slice(block * HD, (block + 1) * HD)
                cosine, sine = cos_sin(where[:, cut], tab[0:HALF, :], tab[HALF : 2 * HALF, :])
                lower, upper = raw[0:HALF, cut], raw[HALF:HD, cut]
                keys[b, 0:HALF, cut] = (lower * cosine - upper * sine).astype(BF16)
                keys[b, HALF:HD, cut] = (upper * cosine + lower * sine).astype(BF16)
        return 0

    cuts = [round(key_steps * f) for f in KEY_CUTS]
    lax.fori_loop(0, cuts[0], build_keys, 0)
    wait_recv(0, a_sib_in)
    both_cores = part[:, core] + unpacked(a_sib_in[...])
    part[:, core] = both_cores
    a_out[...] = packed(both_cores)
    to_chips(1, lambda peer: a_out.at[peer], a_in.at[chip])
    lax.fori_loop(cuts[0], cuts[1], build_keys, 0)

    wait_recv(1, a_in.at[pl.ds(0, chips - 1)])
    total = lax.fori_loop(1, chips, lambda k, t: t + unpacked(a_in[lax.rem(chip + k, chips)]), part[chip, core])
    mean_square = total[64:72] * (1.0 / width)
    projected = total[0:64].reshape(GROUP, 8, HD) * lax.rsqrt(mean_square + NORM_EPSILON)[None]
    step = me // per_step
    first_request = (me - step * per_step) * 8
    sublane = lax.broadcasted_iota(jnp.int32, (8, HD), 0)
    lane = lax.broadcasted_iota(jnp.int32, (8, HD), 1)
    where = jnp.zeros((8, HD), jnp.int32)
    for r in range(8):
        where = jnp.where(sublane == r, start_ref[first_request + r] + step, where)
    cosine, sine = cos_sin(where.astype(F32), tab[HD : HD + 1, :], tab[HD + 1 : HD + 2, :])
    sine = jnp.where(lane < HALF, -sine, sine)
    flat = projected.reshape(64, HD)
    turned = pltpu.roll(flat, HALF, 1).reshape(GROUP, 8, HD)
    queries = (projected * cosine[None] + turned * sine[None]) * HD ** (-0.5)
    row_f32[...] = queries.reshape(64, HD)
    by_request = [row_f32[pl.ds(r, 8, stride=8), :] for r in range(8)]
    q_all[core, chip] = jnp.concatenate(by_request, axis=0).astype(BF16)
    mine = q_all.at[core, chip]
    to_chips(2, lambda peer: mine, mine)
    lax.fori_loop(cuts[1], cuts[2], build_keys, 0)
    wait_recv(2, q_all.at[0, pl.ds(0, chips - 1)])
    copy_to(q_all.at[core], q_all.at[core], 3, sibling, hd).start()
    lax.fori_loop(cuts[2], key_steps, build_keys, 0)
    wait_recv(3, q_all.at[0])

    slot = lax.broadcasted_iota(jnp.int32, (1, slots), 1) + me * slots
    row64 = lax.broadcasted_iota(jnp.int32, (64, HD), 0)
    lane64 = lax.broadcasted_iota(jnp.int32, (64, HD), 1)
    row16 = lax.broadcasted_iota(jnp.int32, (16, HD), 0)

    def queries_of(o):
        tile = o * pair // 8
        inside = pl.multiple_of((o * pair - tile * 8) * 8, 16)
        both = []
        for t in range(steps):
            from_rows = t * per_step + tile
            both.append(q_all[lax.rem(from_rows, 2), from_rows // 2, pl.ds(inside, 8 * pair), :].astype(F32))
        return [jnp.concatenate([x[8 * j : 8 * j + 8] for x in both], axis=0).astype(BF16) for j in range(pair)]

    def attend(owners):
        queries = [q for o in owners for q in queries_of(o)]
        requests_here = [o * pair + j for o in owners for j in range(pair)]
        scores = [jnp.dot(q, keys[b], preferred_element_type=F32) for q, b in zip(queries, requests_here)]
        live = [slot < len_ref[b] for b in requests_here]
        scores = [jnp.where(ok, x, DEAD) for ok, x in zip(live, scores)]
        tops = [jnp.max(x, axis=1, keepdims=True) for x in scores]
        exponents = [jnp.where(ok, jnp.exp(x - top), 0.0) for ok, x, top in zip(live, scores, tops)]
        totals = [jnp.sum(x, axis=1, keepdims=True) for x in exponents]
        mixes = [jnp.dot(x.astype(BF16), val[b], preferred_element_type=F32) for x, b in zip(exponents, requests_here)]
        return [
            [jnp.concatenate(x[pair * i : pair * (i + 1)], axis=0) for x in (mixes, tops, totals)]
            for i in range(len(owners))
        ]

    def message(mix, top, total):
        stats = jnp.where(lane64 == row64, top, jnp.where(lane64 == row64 + HALF, total, 0.0))
        stats = jnp.sum(stats, axis=0, keepdims=True)
        high = stats.astype(BF16).astype(F32)
        middle = (stats - high).astype(BF16).astype(F32)
        low = stats - high - middle
        tail = jnp.where(row16 == 0, high, jnp.where(row16 == 1, middle, jnp.where(row16 == 2, low, 0.0)))
        return jnp.concatenate([mix, tail], axis=0).astype(BF16)

    def merged(mine, block):
        mix, top, total = mine
        block = block.astype(F32)
        stats = jnp.sum(block[64:80], axis=0, keepdims=True)
        their_top = jnp.sum(jnp.where(lane64 == row64, stats, 0.0), axis=1, keepdims=True)
        their_total = jnp.sum(jnp.where(lane64 == row64 + HALF, stats, 0.0), axis=1, keepdims=True)
        both = jnp.maximum(top, their_top)
        ours, theirs = jnp.exp(top - both), jnp.exp(their_top - both)
        return mix * ours + block[0:64] * theirs, both, total * ours + their_total * theirs

    for i in range(CHUNKS):
        big_load(val_hbm, val, val_sem, i).wait()
    batch = chips // 4

    def for_sibling(i, _):
        ks = [i * batch + u for u in range(batch)]
        found = attend([chip_at(k) * 2 + other for k in ks])
        for k, mine in zip(ks, found):
            o_sib_out[k] = message(*mine)
        sent = pl.ds(i * batch, batch)
        pltpu.make_async_remote_copy(
            src_ref=o_sib_out.at[sent], dst_ref=o_sib_in.at[sent], send_sem=send_sem.at[5], recv_sem=batch_sem.at[i],
            device_id=(sibling, hd), device_id_type=MESH,
        ).start()
        return 0

    def for_chips(i, _):
        ks = [i * batch + u for u in range(batch)]
        to = [chip_at(k) for k in ks]
        found = attend([peer * 2 + core for peer in to])
        came = o_sib_in.at[pl.ds(i * batch, batch)]
        pltpu.make_async_remote_copy(
            src_ref=came, dst_ref=came, send_sem=send_sem.at[5], recv_sem=batch_sem.at[i],
            device_id=(sibling, hd), device_id_type=MESH,
        ).wait_recv()
        for k, peer, mine in zip(ks, to, found):
            o_out[peer] = message(*merged(mine, o_sib_in[k]))
        for peer in to[:-1]:
            copy_to(o_out.at[peer], o_in.at[chip], 4, peer * 2 + core, hd).start()

        @pl.when(i < 3)
        def _():
            copy_to(o_out.at[to[-1]], o_in.at[chip], 4, to[-1] * 2 + core, hd).start()

        return 0

    lax.fori_loop(0, 4, for_sibling, 0)
    lax.fori_loop(0, 4, for_chips, 0)
    o_in[chip] = o_out[chip]
    wait_recv(4, o_in.at[pl.ds(0, chips - 1)])
    stats = jnp.sum(o_in[:, 64:80, :].astype(F32), axis=1)
    is_top = lax.broadcasted_iota(jnp.int32, (chips, HD), 1) < HALF
    scale = jnp.where(is_top, jnp.exp(jnp.minimum(stats - jnp.max(stats, axis=0, keepdims=True), 0.0)), 0.0)
    row_total = jnp.sum(scale * pltpu.roll(stats, HALF, 1), axis=0, keepdims=True)
    share = jnp.where(is_top, scale / jnp.where(is_top[0:1], row_total, 1.0), 0.0).T
    mixed = jnp.zeros((64, HD), F32)
    for k in range(chips):
        mixed = mixed + share[0:64, k : k + 1] * o_in[k, 0:64].astype(F32)
    row_f32[...] = mixed
    by_head = [row_f32[pl.ds(g, 8, stride=8), :] for g in range(GROUP)]
    d_all[core, chip] = jnp.concatenate(by_head, axis=0).astype(BF16)
    own_rows = d_all.at[core, chip]
    to_chips(6, lambda peer: own_rows, own_rows)
    wait_recv(6, d_all.at[0, pl.ds(0, chips - 1)])
    copy_to(d_all.at[core], d_all.at[core], 7, sibling, hd).start()

    pieces = m // 2

    def project(side_of):
        wide = d_all[side_of].astype(F32)
        wide = [wide[:, g * 8 : (g + 1) * 8, :].reshape(half_rows, HD) for g in range(GROUP)]
        wide = jnp.concatenate(wide, axis=1).astype(BF16)
        term = jnp.dot(wide, wo[...], preferred_element_type=F32).reshape(pieces, rows // m, wo.shape[1])
        e_f32[pl.ds(side_of * pieces, pieces)] = term
        e_out[pl.ds(side_of * pieces, pieces)] = term.astype(BF16)
        for j in range(pieces):
            to = side_of * pieces + lax.rem(hd + pieces // 2 + j, pieces)

            @pl.when(to != hd)
            def _():
                copy_to(e_out.at[to], e_in.at[lax.rem(hd - to - 1 + m, m)], 8, me, to).start()

    project(core)
    wait_recv(7, d_all.at[0])
    project(other)
    wait_recv(8, e_in)
    total = e_f32[hd]
    for k in range(m - 1):
        total = total + e_in[k].astype(F32)
    y_all[hd] = total.astype(BF16)

    def to_head(k, _):
        copy_to(y_all.at[hd], y_all.at[hd], 9, me, head_at(k)).start()
        return 0

    lax.fori_loop(0, m - 1, to_head, 0)
    wait_recv(9, y_all.at[pl.ds(0, m - 1)])
    gathered = y_all[...].astype(F32).reshape(rows, wo.shape[1])
    for strip in range(wo.shape[1] // HD):
        cut = slice(strip * HD, (strip + 1) * HD)
        y_f32[strip] = gathered[:, cut]
        for c in range(2):
            for j in range(pair):
                for t in range(steps):
                    block = y_f32[strip, pl.ds(c * half_rows + j * steps + t, chips, stride=8), :]
                    y_rows[strip, pl.ds(t * requests + c * pair + j, chips, stride=2 * pair), :] = block
        out_ref[:, cut] = y_rows[strip].astype(BF16)

    wait_send(0, a_sib_in)
    wait_send(1, a_in.at[pl.ds(0, chips - 1)])
    wait_send(2, q_all.at[0, pl.ds(0, chips - 1)])
    wait_send(3, q_all.at[0])
    wait_send(4, o_in.at[pl.ds(0, chips - 1)])
    wait_send(5, o_sib_in)
    wait_send(6, d_all.at[0, pl.ds(0, chips - 1)])
    wait_send(7, d_all.at[0])
    wait_send(8, e_in)
    wait_send(9, y_all.at[pl.ds(0, m - 1)])


def solution(mesh):
    n, m = mesh.shape["seq"], mesh.shape["head"]

    def per_device(hidden_rows, norm_gain, w_query, key_up, key_factors, values, w_out, lengths, key_positions, query_start):
        steps, requests, features = hidden_rows.shape
        rows = steps * requests
        slots, rank = key_factors.shape[2], key_factors.shape[1]
        columns = w_out.shape[1]
        table = turn_tables()
        vmem, sem = pltpu.VMEM, pltpu.SemaphoreType.DMA
        hbm = pl.BlockSpec(memory_space=pl.ANY)
        y = pl.pallas_call(
            functools.partial(kernel, n, m, steps, requests, features * n),
            out_shape=pltpu.VMEM((rows, columns), BF16),
            in_specs=[hbm] * 11,
            out_specs=pl.BlockSpec(memory_space=vmem),
            scratch_shapes=[
                vmem((rows, features), BF16),
                vmem((features,), BF16),
                vmem(w_query.shape, BF16),
                vmem(key_up.shape, BF16),
                vmem((requests, rank, slots), BF16),
                vmem((requests, slots, HD), BF16),
                vmem(w_out.shape, BF16),
                vmem((requests, slots), jnp.int32),
                vmem(table.shape, F32),
                vmem((requests, HD, slots), BF16),
                vmem((n // 2, 2, 72, HD), F32),
                vmem((n // 2, 80, HD), BF16),
                vmem((n // 2, 80, HD), BF16),
                vmem((n // 2, 80, HD), BF16),
                vmem((n // 2, 80, HD), BF16),
                vmem((64, HD), F32),
                vmem((2, n // 2, 64, HD), BF16),
                vmem((n // 2, 80, HD), BF16),
                vmem((n // 2, 80, HD), BF16),
                vmem((n // 2, 80, HD), BF16),
                vmem((n // 2, 80, HD), BF16),
                vmem((2, n // 2, 64, HD), BF16),
                vmem((m, rows // m, columns), F32),
                vmem((m, rows // m, columns), BF16),
                vmem((m - 1, rows // m, columns), BF16),
                vmem((m, rows // m, columns), BF16),
                vmem((columns // HD, rows, HD), F32),
                vmem((columns // HD, rows, HD), F32),
                pltpu.SMEM((requests,), jnp.int32),
                pltpu.SMEM((requests,), jnp.int32),
                sem((9,)),
                sem((CHUNKS,)),
                sem((CHUNKS,)),
                sem((4,)),
                sem((10,)),
                sem((10,)),
            ],
            compiler_params=pltpu.CompilerParams(
                collective_id=0, has_side_effects=True, vmem_limit_bytes=56 * 2**20
            ),
            name="decode",
        )(
            hidden_rows.reshape(rows, features), norm_gain, w_query, key_up, key_factors,
            values, w_out, lengths, key_positions, query_start, jnp.asarray(table),
        )
        return y.reshape(steps, requests, columns)

    return jax.shard_map(
        per_device,
        mesh=mesh,
        in_specs=(
            P(None, None, "seq"),
            P("seq"),
            P("seq", "head"),
            P(None, "head"),
            P(None, None, "seq"),
            P(None, "seq", "head"),
            P("head", "seq"),
            P(),
            P(None, "seq"),
            P(),
        ),
        out_specs=P(None, None, "seq"),
        check_vma=False,
    )
```

```python
import functools
import math

import jax
import jax.numpy as jnp
import numpy as np
from jax import lax
from jax.experimental import pallas as pl
from jax.experimental.pallas import tpu as pltpu
from jax.sharding import PartitionSpec as P

HD = 128
HALF = 64
GROUP = 8
ROPE_BASE = 500000.0
NORM_EPSILON = 1e-05
DEAD = -1e30
MESH = pl.DeviceIdType.MESH
BF16 = jnp.bfloat16
F32 = jnp.float32
UNROLL = 4
KEY_CUTS = (0.125, 0.5, 0.875)
CHUNKS = 4


def turn_tables():
    turns = ROPE_BASE ** (-2.0 * np.arange(HALF) / HD) / (2 * np.pi)
    mantissa, power = np.frexp(turns)
    head = np.ldexp(np.round(mantissa * 512) / 512, power)
    tail = turns - head
    rows = np.zeros((8, HD))
    rows[0], rows[1] = np.tile(head, 2), np.tile(tail, 2)
    columns = [np.broadcast_to(v[:, None], (HALF, HD)) for v in (head, tail)]
    return np.concatenate([*columns, rows]).astype(np.float32)


def chebyshev(function, terms):
    fit = np.polynomial.chebyshev.Chebyshev.interpolate(function, terms - 1, domain=[0, 0.25])
    return fit.convert(kind=np.polynomial.Polynomial).coef


COSINE = chebyshev(lambda z: np.cos(2 * np.pi * np.sqrt(z)), 6)
SINE = chebyshev(lambda z: 2 * np.pi * np.sinc(2 * np.sqrt(z)), 5)


def horner(coefficients, z):
    total = z * float(coefficients[-1]) + float(coefficients[-2])
    for c in coefficients[-3::-1]:
        total = total * z + float(c)
    return total


def cos_sin(position, head, tail):
    coarse, fine = position * head, position * tail
    part = (coarse - jnp.round(coarse + fine)) + fine
    square = part * part
    return horner(COSINE, square), part * horner(SINE, square)


def far_first(k, size):
    return (2 + k + (k * (k - 1)) // 2) % 4 if size == 4 else (k + 1) % size


def kernel(
    n, m, steps, requests, width,
    hid_hbm, gain_hbm, wq_hbm, ku_hbm, fac_hbm, val_hbm, wo_hbm, len_hbm, pos_hbm, start_hbm, tab_hbm,
    out_ref,
    hid, gain, wq, ku, fac, val, wo, pos, tab, keys,
    scaled, square_f32, part, a_sib_out, a_sib_in, a_out, a_in, row_f32, q_all, o_sib_out, o_sib_in, o_out, o_in, d_all, e_f32, e_out, e_in, y_all,
    y_f32, y_rows, len_ref, start_ref, load_sem, fac_sem, val_sem, batch_sem, send_sem, recv_sem,
):
    me, hd = lax.axis_index("seq"), lax.axis_index("head")
    chip, core = me // 2, lax.rem(me, 2)
    other = 1 - core
    sibling = chip * 2 + other
    chips = n // 2
    side = math.isqrt(chips)
    slots = fac.shape[2]
    rows = steps * requests
    pair = requests // n
    per_step = requests // 8
    half_rows = rows // 2

    x, y = chip // side, lax.rem(chip, side)

    def chip_at(k):
        over = lax.rem(x + far_first(k // side, side), side) * side
        return over + lax.rem(y + far_first(k % side, side), side)

    def head_at(k):
        away = (k + 1) // 2
        return lax.rem(hd + m + m // 2 + (-away if k % 2 else away), m)

    def copy_to(src, dst, phase, peer, head):
        return pltpu.make_async_remote_copy(
            src_ref=src, dst_ref=dst, send_sem=send_sem.at[phase], recv_sem=recv_sem.at[phase],
            device_id=(peer, head), device_id_type=MESH,
        )

    def to_chips(phase, src_of, dst):
        for k in range(chips - 1):
            peer = chip_at(k)
            copy_to(src_of(peer), dst, phase, peer * 2 + core, hd).start()

    def wait_recv(phase, ref):
        copy_to(ref, ref, phase, sibling, hd).wait_recv()

    def wait_send(phase, ref):
        copy_to(ref, ref, phase, sibling, hd).wait_send()

    first = [(hid_hbm, hid), (gain_hbm, gain), (wq_hbm, wq), (tab_hbm, tab), (ku_hbm, ku), (pos_hbm, pos), (wo_hbm, wo)]
    first += [(len_hbm, len_ref), (start_hbm, start_ref)]
    loads = [pltpu.make_async_copy(src, dst, load_sem.at[i]) for i, (src, dst) in enumerate(first)]
    for copy in loads[:3]:
        copy.start()

    barrier = pltpu.get_barrier_semaphore()

    def greet(peer, head):
        pl.semaphore_signal(barrier, inc=1, device_id=(peer, head), device_id_type=MESH)

    for k in range(m - 1):
        greet(me, head_at(k))
    for k in range(chips - 1):
        greet(chip_at(k) * 2 + core, hd)
    greet(sibling, hd)
    for copy in loads[3:]:
        copy.start()

    def big_load(src, dst, sem, i):
        block = pl.ds(i * (requests // CHUNKS), requests // CHUNKS)
        return pltpu.make_async_copy(src.at[block], dst.at[block], sem.at[i])

    key_steps = requests // UNROLL
    chunk_steps = key_steps // CHUNKS
    for i in range(CHUNKS):
        big_load(fac_hbm, fac, fac_sem, i).start()

    for copy in loads[:3]:
        copy.wait()
    widened = hid[...].astype(F32)
    squares = jnp.sum(widened * widened, axis=-1, keepdims=True)
    squares = jnp.broadcast_to(squares, (rows, HD)).reshape(chips, 2, 8, HD)
    scaled[...] = (widened * gain[...].astype(F32).reshape(1, -1)).reshape(scaled.shape)
    square_f32[...] = squares

    def terms(side_of):
        normed = scaled[:, side_of].reshape(half_rows, scaled.shape[3]).astype(BF16)
        found = []
        for g in range(0, GROUP, 2):
            term = jnp.dot(normed, wq[:, g * HD : (g + 2) * HD], preferred_element_type=F32)
            found += [term[:, 0:HD].reshape(chips, 8, HD), term[:, HD : 2 * HD].reshape(chips, 8, HD)]
        return jnp.concatenate([*found, square_f32[:, side_of]], axis=1)

    def packed(block):
        square = block[:, 64:72]
        head = square.astype(BF16).astype(F32)
        return jnp.concatenate([block[:, 0:64], head, square - head], axis=1).astype(BF16)

    def unpacked(block):
        block = block.astype(F32)
        return jnp.concatenate([block[..., 0:64, :], block[..., 64:72, :] + block[..., 72:80, :]], axis=-2)

    a_sib_out[...] = packed(terms(other))
    pl.semaphore_wait(barrier, chips + m - 1)
    copy_to(a_sib_out, a_sib_in, 0, sibling, hd).start()
    part[...] = terms(core)

    for copy in loads[3:]:
        copy.wait()
    up_rows = ku[...].T

    def build_keys(i, _):
        @pl.when(lax.rem(i, chunk_steps) == 0)
        def _():
            big_load(fac_hbm, fac, fac_sem, i // chunk_steps).wait()

        for u in range(UNROLL):
            b = i * UNROLL + u
            raw = jnp.dot(up_rows, fac[b], preferred_element_type=F32)
            where = pos[pl.ds(b, 1), :].astype(F32)
            for block in range(slots // HD):
                cut = slice(block * HD, (block + 1) * HD)
                cosine, sine = cos_sin(where[:, cut], tab[0:HALF, :], tab[HALF : 2 * HALF, :])
                lower, upper = raw[0:HALF, cut], raw[HALF:HD, cut]
                keys[b, 0:HALF, cut] = (lower * cosine - upper * sine).astype(BF16)
                keys[b, HALF:HD, cut] = (upper * cosine + lower * sine).astype(BF16)
        return 0

    cuts = [round(key_steps * f) for f in KEY_CUTS]
    lax.fori_loop(0, cuts[0], build_keys, 0)
    wait_recv(0, a_sib_in)
    both_cores = part[...] + unpacked(a_sib_in[...])
    part[...] = both_cores
    a_out[...] = packed(both_cores)
    to_chips(1, lambda peer: a_out.at[peer], a_in.at[chip])
    for i in range(CHUNKS):
        big_load(val_hbm, val, val_sem, i).start()
    lax.fori_loop(cuts[0], cuts[1], build_keys, 0)

    wait_recv(1, a_in.at[pl.ds(0, chips - 1)])
    total = lax.fori_loop(1, chips, lambda k, t: t + unpacked(a_in[lax.rem(chip + k, chips)]), part[chip])
    mean_square = total[64:72] * (1.0 / width)
    projected = total[0:64].reshape(GROUP, 8, HD) * lax.rsqrt(mean_square + NORM_EPSILON)[None]
    step = me // per_step
    first_request = (me - step * per_step) * 8
    sublane = lax.broadcasted_iota(jnp.int32, (8, HD), 0)
    lane = lax.broadcasted_iota(jnp.int32, (8, HD), 1)
    where = jnp.zeros((8, HD), jnp.int32)
    for r in range(8):
        where = jnp.where(sublane == r, start_ref[first_request + r] + step, where)
    cosine, sine = cos_sin(where.astype(F32), tab[HD : HD + 1, :], tab[HD + 1 : HD + 2, :])
    sine = jnp.where(lane < HALF, -sine, sine)
    flat = projected.reshape(64, HD)
    turned = pltpu.roll(flat, HALF, 1).reshape(GROUP, 8, HD)
    queries = (projected * cosine[None] + turned * sine[None]) * HD ** (-0.5)
    row_f32[...] = queries.reshape(64, HD)
    by_request = [row_f32[pl.ds(r, 8, stride=8), :] for r in range(8)]
    q_all[core, chip] = jnp.concatenate(by_request, axis=0).astype(BF16)
    mine = q_all.at[core, chip]
    to_chips(2, lambda peer: mine, mine)
    lax.fori_loop(cuts[1], cuts[2], build_keys, 0)
    wait_recv(2, q_all.at[0, pl.ds(0, chips - 1)])
    copy_to(q_all.at[core], q_all.at[core], 3, sibling, hd).start()
    lax.fori_loop(cuts[2], key_steps, build_keys, 0)
    wait_recv(3, q_all.at[0])

    slot = lax.broadcasted_iota(jnp.int32, (1, slots), 1) + me * slots
    row64 = lax.broadcasted_iota(jnp.int32, (1, 64, HD), 1)
    lane64 = lax.broadcasted_iota(jnp.int32, (1, 64, HD), 2)
    row16 = lax.broadcasted_iota(jnp.int32, (1, 16, HD), 1)

    def queries_of(o):
        tile = o * pair // 8
        inside = pl.multiple_of((o * pair - tile * 8) * 8, 16)
        both = []
        for t in range(steps):
            from_rows = t * per_step + tile
            both.append(q_all[lax.rem(from_rows, 2), from_rows // 2, pl.ds(inside, 8 * pair), :].astype(F32))
        return [jnp.concatenate([x[8 * j : 8 * j + 8] for x in both], axis=0).astype(BF16) for j in range(pair)]

    def attend(owners):
        queries = [q for o in owners for q in queries_of(o)]
        requests_here = [o * pair + j for o in owners for j in range(pair)]
        scores = [jnp.dot(q, keys[b], preferred_element_type=F32) for q, b in zip(queries, requests_here)]
        live = [slot < len_ref[b] for b in requests_here]
        scores = [jnp.where(ok, x, DEAD) for ok, x in zip(live, scores)]
        tops = [jnp.max(x, axis=1, keepdims=True) for x in scores]
        exponents = [jnp.where(ok, jnp.exp(x - top), 0.0) for ok, x, top in zip(live, scores, tops)]
        totals = [jnp.sum(x, axis=1, keepdims=True) for x in exponents]
        mixes = [jnp.dot(x.astype(BF16), val[b], preferred_element_type=F32) for x, b in zip(exponents, requests_here)]
        return [jnp.concatenate(x, axis=0).reshape(len(owners), 64, -1) for x in (mixes, tops, totals)]

    def message(mix, top, total):
        stats = jnp.where(lane64 == row64, top, jnp.where(lane64 == row64 + HALF, total, 0.0))
        stats = jnp.sum(stats, axis=1, keepdims=True)
        high = stats.astype(BF16).astype(F32)
        middle = (stats - high).astype(BF16).astype(F32)
        low = stats - high - middle
        tail = jnp.where(row16 == 0, high, jnp.where(row16 == 1, middle, jnp.where(row16 == 2, low, 0.0)))
        return jnp.concatenate([mix, tail], axis=1).astype(BF16)

    def merged(mine, blocks):
        mix, top, total = mine
        blocks = blocks.astype(F32)
        stats = jnp.sum(blocks[:, 64:80], axis=1, keepdims=True)
        their_top = jnp.sum(jnp.where(lane64 == row64, stats, 0.0), axis=2, keepdims=True)
        their_total = jnp.sum(jnp.where(lane64 == row64 + HALF, stats, 0.0), axis=2, keepdims=True)
        both = jnp.maximum(top, their_top)
        ours, theirs = jnp.exp(top - both), jnp.exp(their_top - both)
        return mix * ours + blocks[:, 0:64] * theirs, both, total * ours + their_total * theirs

    for i in range(CHUNKS):
        big_load(val_hbm, val, val_sem, i).wait()
    batch = chips // 4

    def owners_at(i):
        return [chip_at(i * batch + u) for u in range(batch)]

    def for_sibling(i, _):
        found = attend([peer * 2 + other for peer in owners_at(i)])
        sent = pl.ds(i * batch, batch)
        o_sib_out[sent] = message(*found)
        pltpu.make_async_remote_copy(
            src_ref=o_sib_out.at[sent], dst_ref=o_sib_in.at[sent], send_sem=send_sem.at[5], recv_sem=batch_sem.at[i],
            device_id=(sibling, hd), device_id_type=MESH,
        ).start()
        return 0

    def for_chips(i, _):
        to = owners_at(i)
        found = attend([peer * 2 + core for peer in to])
        came = o_sib_in.at[pl.ds(i * batch, batch)]
        pltpu.make_async_remote_copy(
            src_ref=came, dst_ref=came, send_sem=send_sem.at[5], recv_sem=batch_sem.at[i],
            device_id=(sibling, hd), device_id_type=MESH,
        ).wait_recv()
        blocks = message(*merged(found, came[...]))
        for u, peer in enumerate(to):
            o_out[peer] = blocks[u]
        for peer in to[:-1]:
            copy_to(o_out.at[peer], o_in.at[chip], 4, peer * 2 + core, hd).start()

        @pl.when(i < 3)
        def _():
            copy_to(o_out.at[to[-1]], o_in.at[chip], 4, to[-1] * 2 + core, hd).start()

        return 0

    lax.fori_loop(0, 4, for_sibling, 0)
    lax.fori_loop(0, 4, for_chips, 0)
    o_in[chip] = o_out[chip]
    wait_recv(4, o_in.at[pl.ds(0, chips - 1)])
    stats = jnp.sum(o_in[:, 64:80, :].astype(F32), axis=1)
    is_top = lax.broadcasted_iota(jnp.int32, (chips, HD), 1) < HALF
    scale = jnp.where(is_top, jnp.exp(jnp.minimum(stats - jnp.max(stats, axis=0, keepdims=True), 0.0)), 0.0)
    row_total = jnp.sum(scale * pltpu.roll(stats, HALF, 1), axis=0, keepdims=True)
    share = jnp.where(is_top, scale / jnp.where(is_top[0:1], row_total, 1.0), 0.0).T
    mixed = jnp.zeros((64, HD), F32)
    for k in range(chips):
        mixed = mixed + share[0:64, k : k + 1] * o_in[k, 0:64].astype(F32)
    row_f32[...] = mixed
    by_head = [row_f32[pl.ds(g, 8, stride=8), :] for g in range(GROUP)]
    d_all[core, chip] = jnp.concatenate(by_head, axis=0).astype(BF16)
    own_rows = d_all.at[core, chip]
    to_chips(6, lambda peer: own_rows, own_rows)
    wait_recv(6, d_all.at[0, pl.ds(0, chips - 1)])
    copy_to(d_all.at[core], d_all.at[core], 7, sibling, hd).start()

    pieces = m // 2

    def project(side_of):
        wide = d_all[side_of].astype(F32)
        wide = [wide[:, g * 8 : (g + 1) * 8, :].reshape(half_rows, HD) for g in range(GROUP)]
        wide = jnp.concatenate(wide, axis=1).astype(BF16)
        term = jnp.dot(wide, wo[...], preferred_element_type=F32).reshape(pieces, rows // m, wo.shape[1])
        e_f32[pl.ds(side_of * pieces, pieces)] = term
        e_out[pl.ds(side_of * pieces, pieces)] = term.astype(BF16)
        for j in range(pieces):
            to = side_of * pieces + lax.rem(hd + pieces // 2 + j, pieces)

            @pl.when(to != hd)
            def _():
                copy_to(e_out.at[to], e_in.at[lax.rem(hd - to - 1 + m, m)], 8, me, to).start()

    project(core)
    wait_recv(7, d_all.at[0])
    project(other)
    wait_recv(8, e_in)
    total = e_f32[hd]
    for k in range(m - 1):
        total = total + e_in[k].astype(F32)
    y_all[hd] = total.astype(BF16)

    for k in range(m - 1):
        copy_to(y_all.at[hd], y_all.at[hd], 9, me, head_at(k)).start()
    wait_recv(9, y_all.at[pl.ds(0, m - 1)])
    gathered = y_all[...].astype(F32).reshape(rows, wo.shape[1])
    for strip in range(wo.shape[1] // HD):
        cut = slice(strip * HD, (strip + 1) * HD)
        y_f32[strip] = gathered[:, cut]
        for c in range(2):
            for j in range(pair):
                for t in range(steps):
                    block = y_f32[strip, pl.ds(c * half_rows + j * steps + t, chips, stride=8), :]
                    y_rows[strip, pl.ds(t * requests + c * pair + j, chips, stride=2 * pair), :] = block
        out_ref[:, cut] = y_rows[strip].astype(BF16)

    wait_send(0, a_sib_in)
    wait_send(1, a_in.at[pl.ds(0, chips - 1)])
    wait_send(2, q_all.at[0, pl.ds(0, chips - 1)])
    wait_send(3, q_all.at[0])
    wait_send(4, o_in.at[pl.ds(0, chips - 1)])
    wait_send(5, o_sib_in)
    wait_send(6, d_all.at[0, pl.ds(0, chips - 1)])
    wait_send(7, d_all.at[0])
    wait_send(8, e_in)
    wait_send(9, y_all.at[pl.ds(0, m - 1)])


def solution(mesh):
    n, m = mesh.shape["seq"], mesh.shape["head"]

    def per_device(hidden_rows, norm_gain, w_query, key_up, key_factors, values, w_out, lengths, key_positions, query_start):
        steps, requests, features = hidden_rows.shape
        rows = steps * requests
        slots, rank = key_factors.shape[2], key_factors.shape[1]
        columns = w_out.shape[1]
        table = turn_tables()
        vmem, sem = pltpu.VMEM, pltpu.SemaphoreType.DMA
        hbm = pl.BlockSpec(memory_space=pl.ANY)
        y = pl.pallas_call(
            functools.partial(kernel, n, m, steps, requests, features * n),
            out_shape=pltpu.VMEM((rows, columns), BF16),
            in_specs=[hbm] * 11,
            out_specs=pl.BlockSpec(memory_space=vmem),
            scratch_shapes=[
                vmem((rows, features), BF16),
                vmem((features,), BF16),
                vmem(w_query.shape, BF16),
                vmem(key_up.shape, BF16),
                vmem((requests, rank, slots), BF16),
                vmem((requests, slots, HD), BF16),
                vmem(w_out.shape, BF16),
                vmem((requests, slots), jnp.int32),
                vmem(table.shape, F32),
                vmem((requests, HD, slots), BF16),
                vmem((n // 2, 2, 8, features), F32),
                vmem((n // 2, 2, 8, HD), F32),
                vmem((n // 2, 72, HD), F32),
                vmem((n // 2, 80, HD), BF16),
                vmem((n // 2, 80, HD), BF16),
                vmem((n // 2, 80, HD), BF16),
                vmem((n // 2, 80, HD), BF16),
                vmem((64, HD), F32),
                vmem((2, n // 2, 64, HD), BF16),
                vmem((n // 2, 80, HD), BF16),
                vmem((n // 2, 80, HD), BF16),
                vmem((n // 2, 80, HD), BF16),
                vmem((n // 2, 80, HD), BF16),
                vmem((2, n // 2, 64, HD), BF16),
                vmem((m, rows // m, columns), F32),
                vmem((m, rows // m, columns), BF16),
                vmem((m - 1, rows // m, columns), BF16),
                vmem((m, rows // m, columns), BF16),
                vmem((columns // HD, rows, HD), F32),
                vmem((columns // HD, rows, HD), F32),
                pltpu.SMEM((requests,), jnp.int32),
                pltpu.SMEM((requests,), jnp.int32),
                sem((9,)),
                sem((CHUNKS,)),
                sem((CHUNKS,)),
                sem((4,)),
                sem((10,)),
                sem((10,)),
            ],
            compiler_params=pltpu.CompilerParams(
                collective_id=0, has_side_effects=True, vmem_limit_bytes=56 * 2**20
            ),
            name="decode",
        )(
            hidden_rows.reshape(rows, features), norm_gain, w_query, key_up, key_factors,
            values, w_out, lengths, key_positions, query_start, jnp.asarray(table),
        )
        return y.reshape(steps, requests, columns)

    return jax.shard_map(
        per_device,
        mesh=mesh,
        in_specs=(
            P(None, None, "seq"),
            P("seq"),
            P("seq", "head"),
            P(None, "head"),
            P(None, None, "seq"),
            P(None, "seq", "head"),
            P("head", "seq"),
            P(),
            P(None, "seq"),
            P(),
        ),
        out_specs=P(None, None, "seq"),
        check_vma=False,
    )
```

```python
import functools
import math

import jax
import jax.numpy as jnp
import numpy as np
from jax import lax
from jax.experimental import pallas as pl
from jax.experimental.pallas import tpu as pltpu
from jax.sharding import PartitionSpec as P

HD = 128
HALF = 64
GROUP = 8
ROPE_BASE = 500000.0
NORM_EPSILON = 1e-05
DEAD = -1e30
MESH = pl.DeviceIdType.MESH
BF16 = jnp.bfloat16
F32 = jnp.float32
UNROLL = 4
KEY_CUTS = (0.0625, 0.5, 0.875)
CHUNKS = 4


def turn_tables():
    turns = ROPE_BASE ** (-2.0 * np.arange(HALF) / HD) / (2 * np.pi)
    mantissa, power = np.frexp(turns)
    head = np.ldexp(np.round(mantissa * 512) / 512, power)
    tail = turns - head
    rows = np.zeros((8, HD))
    rows[0], rows[1] = np.tile(head, 2), np.tile(tail, 2)
    columns = [np.broadcast_to(v[:, None], (HALF, HD)) for v in (head, tail)]
    return np.concatenate([*columns, rows]).astype(np.float32)


def chebyshev(function, terms):
    fit = np.polynomial.chebyshev.Chebyshev.interpolate(function, terms - 1, domain=[0, 0.25])
    return fit.convert(kind=np.polynomial.Polynomial).coef


COSINE = chebyshev(lambda z: np.cos(2 * np.pi * np.sqrt(z)), 6)
SINE = chebyshev(lambda z: 2 * np.pi * np.sinc(2 * np.sqrt(z)), 5)


def horner(coefficients, z):
    total = z * float(coefficients[-1]) + float(coefficients[-2])
    for c in coefficients[-3::-1]:
        total = total * z + float(c)
    return total


def cos_sin(position, head, tail):
    coarse, fine = position * head, position * tail
    part = (coarse - jnp.round(coarse + fine)) + fine
    square = part * part
    return horner(COSINE, square), part * horner(SINE, square)


def far_first(side):
    def hops(d):
        return min(d, side - d)

    places = [(x, y) for x in range(side) for y in range(side)]
    places.sort(key=lambda p: -hops(p[0]) - hops(p[1]))
    return [x * side + y for x, y in places]


def kernel(
    n, m, steps, requests, width,
    hid_hbm, gain_hbm, wq_hbm, ku_hbm, fac_hbm, val_hbm, wo_hbm, len_hbm, pos_hbm, start_hbm, tab_hbm,
    out_ref,
    hid, gain, wq, ku, fac, val, wo, pos, tab, keys,
    scaled, square_f32, part, a_sib_out, a_sib_in, a_out, a_in, row_f32, q_all, o_sib_out, o_sib_in, o_out, o_in, d_all, e_f32, e_out, e_in, y_all,
    y_f32, y_rows, len_ref, start_ref, load_sem, fac_sem, val_sem, batch_sem, send_sem, recv_sem,
):
    me, hd = lax.axis_index("seq"), lax.axis_index("head")
    chip, core = me // 2, lax.rem(me, 2)
    other = 1 - core
    sibling = chip * 2 + other
    chips = n // 2
    side = math.isqrt(chips)
    slots = fac.shape[2]
    rows = steps * requests
    pair = requests // n
    per_step = requests // 8
    half_rows = rows // 2

    x, y = chip // side, lax.rem(chip, side)

    offsets = far_first(side)
    batch = chips // 4
    digits = [sum(offsets[i * batch + u] * 16**i for i in range(4)) for u in range(batch)]

    def chip_at(offset):
        over = lax.rem(x + lax.div(offset, side), side) * side
        return over + lax.rem(y + lax.rem(offset, side), side)

    near = [lax.rem(x + o // side, side) * side + lax.rem(y + o % side, side) for o in offsets]

    def batch_of(digits):
        return [chip_at(lax.rem(digit, 16)) for digit in digits]

    def after(digits):
        return [lax.div(digit, 16) for digit in digits]

    def head_at(k):
        away = (k + 1) // 2
        return lax.rem(hd + m + m // 2 + (-away if k % 2 else away), m)

    def copy_to(src, dst, phase, peer, head):
        return pltpu.make_async_remote_copy(
            src_ref=src, dst_ref=dst, send_sem=send_sem.at[phase], recv_sem=recv_sem.at[phase],
            device_id=(peer, head), device_id_type=MESH,
        )

    def to_chips(phase, src_of, dst):
        for k in range(chips - 1):
            peer = near[k]
            copy_to(src_of(peer), dst, phase, peer * 2 + core, hd).start()

    def wait_recv(phase, ref):
        copy_to(ref, ref, phase, sibling, hd).wait_recv()

    def wait_send(phase, ref):
        copy_to(ref, ref, phase, sibling, hd).wait_send()

    first = [(hid_hbm, hid), (gain_hbm, gain), (wq_hbm, wq), (tab_hbm, tab), (ku_hbm, ku), (pos_hbm, pos), (wo_hbm, wo)]
    first += [(len_hbm, len_ref), (start_hbm, start_ref)]
    loads = [pltpu.make_async_copy(src, dst, load_sem.at[i]) for i, (src, dst) in enumerate(first)]
    for copy in loads[:3]:
        copy.start()

    barrier = pltpu.get_barrier_semaphore()

    def greet(peer, head):
        pl.semaphore_signal(barrier, inc=1, device_id=(peer, head), device_id_type=MESH)

    for k in range(m - 1):
        greet(me, head_at(k))
    for k in range(chips - 1):
        greet(near[k] * 2 + core, hd)
    greet(sibling, hd)
    for copy in loads[3:]:
        copy.start()

    def big_load(src, dst, sem, i):
        block = pl.ds(i * (requests // CHUNKS), requests // CHUNKS)
        return pltpu.make_async_copy(src.at[block], dst.at[block], sem.at[i])

    key_steps = requests // UNROLL
    chunk_steps = key_steps // CHUNKS
    for i in range(CHUNKS):
        big_load(fac_hbm, fac, fac_sem, i).start()

    for copy in loads[:3]:
        copy.wait()
    widened = hid[...].astype(F32)
    squares = jnp.sum(widened * widened, axis=-1, keepdims=True)
    squares = jnp.broadcast_to(squares, (rows, HD)).reshape(chips, 2, 8, HD)
    scaled[...] = (widened * gain[...].astype(F32).reshape(1, -1)).reshape(scaled.shape)
    square_f32[...] = squares

    def terms(side_of):
        normed = scaled[:, side_of].reshape(half_rows, scaled.shape[3]).astype(BF16)
        found = []
        for g in range(0, GROUP, 2):
            term = jnp.dot(normed, wq[:, g * HD : (g + 2) * HD], preferred_element_type=F32)
            found += [term[:, 0:HD].reshape(chips, 8, HD), term[:, HD : 2 * HD].reshape(chips, 8, HD)]
        return jnp.concatenate([*found, square_f32[:, side_of]], axis=1)

    def packed(block):
        square = block[:, 64:72]
        head = square.astype(BF16).astype(F32)
        return jnp.concatenate([block[:, 0:64], head, square - head], axis=1).astype(BF16)

    def unpacked(block):
        block = block.astype(F32)
        return jnp.concatenate([block[..., 0:64, :], block[..., 64:72, :] + block[..., 72:80, :]], axis=-2)

    a_sib_out[...] = packed(terms(other))
    pl.semaphore_wait(barrier, chips + m - 1)
    copy_to(a_sib_out, a_sib_in, 0, sibling, hd).start()
    part[...] = terms(core)

    for copy in loads[3:]:
        copy.wait()
    up_rows = ku[...].T

    def build_keys(i, _):
        @pl.when(lax.rem(i, chunk_steps) == 0)
        def _():
            big_load(fac_hbm, fac, fac_sem, i // chunk_steps).wait()

        for u in range(UNROLL):
            b = i * UNROLL + u
            raw = jnp.dot(up_rows, fac[b], preferred_element_type=F32)
            where = pos[pl.ds(b, 1), :].astype(F32)
            for block in range(slots // HD):
                cut = slice(block * HD, (block + 1) * HD)
                cosine, sine = cos_sin(where[:, cut], tab[0:HALF, :], tab[HALF : 2 * HALF, :])
                lower, upper = raw[0:HALF, cut], raw[HALF:HD, cut]
                keys[b, 0:HALF, cut] = (lower * cosine - upper * sine).astype(BF16)
                keys[b, HALF:HD, cut] = (upper * cosine + lower * sine).astype(BF16)
        return 0

    cuts = [round(key_steps * f) for f in KEY_CUTS]
    lax.fori_loop(0, cuts[0], build_keys, 0)
    wait_recv(0, a_sib_in)
    both_cores = part[...] + unpacked(a_sib_in[...])
    part[...] = both_cores
    a_out[...] = packed(both_cores)
    to_chips(1, lambda peer: a_out.at[peer], a_in.at[chip])
    for i in range(CHUNKS):
        big_load(val_hbm, val, val_sem, i).start()
    lax.fori_loop(cuts[0], cuts[1], build_keys, 0)

    wait_recv(1, a_in.at[pl.ds(0, chips - 1)])
    total = part[chip]
    for k in range(1, chips):
        total = total + unpacked(a_in[lax.rem(chip + k, chips)])
    mean_square = total[64:72] * (1.0 / width)
    projected = total[0:64].reshape(GROUP, 8, HD) * lax.rsqrt(mean_square + NORM_EPSILON)[None]
    step = me // per_step
    first_request = (me - step * per_step) * 8
    sublane = lax.broadcasted_iota(jnp.int32, (8, HD), 0)
    lane = lax.broadcasted_iota(jnp.int32, (8, HD), 1)
    where = jnp.zeros((8, HD), jnp.int32)
    for r in range(8):
        where = jnp.where(sublane == r, start_ref[first_request + r] + step, where)
    cosine, sine = cos_sin(where.astype(F32), tab[HD : HD + 1, :], tab[HD + 1 : HD + 2, :])
    sine = jnp.where(lane < HALF, -sine, sine)
    flat = projected.reshape(64, HD)
    turned = pltpu.roll(flat, HALF, 1).reshape(GROUP, 8, HD)
    queries = (projected * cosine[None] + turned * sine[None]) * HD ** (-0.5)
    row_f32[...] = queries.reshape(64, HD)
    by_request = [row_f32[pl.ds(r, 8, stride=8), :] for r in range(8)]
    q_all[core, chip] = jnp.concatenate(by_request, axis=0).astype(BF16)
    mine = q_all.at[core, chip]
    to_chips(2, lambda peer: mine, mine)
    lax.fori_loop(cuts[1], cuts[2], build_keys, 0)
    wait_recv(2, q_all.at[0, pl.ds(0, chips - 1)])
    copy_to(q_all.at[core], q_all.at[core], 3, sibling, hd).start()
    lax.fori_loop(cuts[2], key_steps, build_keys, 0)
    wait_recv(3, q_all.at[0])

    slot = lax.broadcasted_iota(jnp.int32, (1, slots), 1) + me * slots
    row64 = lax.broadcasted_iota(jnp.int32, (1, 64, HD), 1)
    lane64 = lax.broadcasted_iota(jnp.int32, (1, 64, HD), 2)
    row16 = lax.broadcasted_iota(jnp.int32, (1, 16, HD), 1)

    def queries_of(o):
        tile = o * pair // 8
        inside = pl.multiple_of((o * pair - tile * 8) * 8, 16)
        both = []
        for t in range(steps):
            from_rows = t * per_step + tile
            both.append(q_all[lax.rem(from_rows, 2), from_rows // 2, pl.ds(inside, 8 * pair), :].astype(F32))
        return [jnp.concatenate([x[8 * j : 8 * j + 8] for x in both], axis=0).astype(BF16) for j in range(pair)]

    def attend(owners):
        queries = [q for o in owners for q in queries_of(o)]
        requests_here = [o * pair + j for o in owners for j in range(pair)]
        scores = [jnp.dot(q, keys[b], preferred_element_type=F32) for q, b in zip(queries, requests_here)]
        live = [slot < len_ref[b] for b in requests_here]
        scores = [jnp.where(ok, x, DEAD) for ok, x in zip(live, scores)]
        tops = [jnp.max(x, axis=1, keepdims=True) for x in scores]
        exponents = [jnp.where(ok, jnp.exp(x - top), 0.0) for ok, x, top in zip(live, scores, tops)]
        totals = [jnp.sum(x, axis=1, keepdims=True) for x in exponents]
        mixes = [jnp.dot(x.astype(BF16), val[b], preferred_element_type=F32) for x, b in zip(exponents, requests_here)]
        return [jnp.concatenate(x, axis=0).reshape(len(owners), 64, -1) for x in (mixes, tops, totals)]

    def message(mix, top, total):
        stats = jnp.where(lane64 == row64, top, jnp.where(lane64 == row64 + HALF, total, 0.0))
        stats = jnp.sum(stats, axis=1, keepdims=True)
        high = stats.astype(BF16).astype(F32)
        middle = (stats - high).astype(BF16).astype(F32)
        low = stats - high - middle
        tail = jnp.where(row16 == 0, high, jnp.where(row16 == 1, middle, jnp.where(row16 == 2, low, 0.0)))
        return jnp.concatenate([mix, tail], axis=1).astype(BF16)

    def merged(mine, blocks):
        mix, top, total = mine
        blocks = blocks.astype(F32)
        stats = jnp.sum(blocks[:, 64:80], axis=1, keepdims=True)
        their_top = jnp.sum(jnp.where(lane64 == row64, stats, 0.0), axis=2, keepdims=True)
        their_total = jnp.sum(jnp.where(lane64 == row64 + HALF, stats, 0.0), axis=2, keepdims=True)
        both = jnp.maximum(top, their_top)
        ours, theirs = jnp.exp(top - both), jnp.exp(their_top - both)
        return mix * ours + blocks[:, 0:64] * theirs, both, total * ours + their_total * theirs

    for i in range(CHUNKS):
        big_load(val_hbm, val, val_sem, i).wait()
    def for_sibling(i, digits):
        found = attend([peer * 2 + other for peer in batch_of(digits) + batch_of(after(digits))])
        sent = pl.ds(i * 2 * batch, 2 * batch)
        o_sib_out[sent] = message(*found)
        pltpu.make_async_remote_copy(
            src_ref=o_sib_out.at[sent], dst_ref=o_sib_in.at[sent], send_sem=send_sem.at[5], recv_sem=batch_sem.at[i],
            device_id=(sibling, hd), device_id_type=MESH,
        ).start()
        return after(after(digits))

    def for_chips(i, digits):
        to = batch_of(digits)
        found = attend([peer * 2 + core for peer in to])

        @pl.when(lax.rem(i, 2) == 0)
        def _():
            came = o_sib_in.at[pl.ds(i * batch, 2 * batch)]
            pltpu.make_async_remote_copy(
                src_ref=came, dst_ref=came, send_sem=send_sem.at[5], recv_sem=batch_sem.at[i // 2],
                device_id=(sibling, hd), device_id_type=MESH,
            ).wait_recv()

        blocks = message(*merged(found, o_sib_in[pl.ds(i * batch, batch)]))
        for u, peer in enumerate(to):
            o_out[peer] = blocks[u]
        for peer in to[:-1]:
            copy_to(o_out.at[peer], o_in.at[chip], 4, peer * 2 + core, hd).start()

        @pl.when(i < 3)
        def _():
            copy_to(o_out.at[to[-1]], o_in.at[chip], 4, to[-1] * 2 + core, hd).start()

        return after(digits)

    digits = [jnp.int32(digit) for digit in digits]
    lax.fori_loop(0, 2, for_sibling, digits)
    lax.fori_loop(0, 4, for_chips, digits)
    o_in[chip] = o_out[chip]
    wait_recv(4, o_in.at[pl.ds(0, chips - 1)])
    stats = jnp.sum(o_in[:, 64:80, :].astype(F32), axis=1)
    is_top = lax.broadcasted_iota(jnp.int32, (chips, HD), 1) < HALF
    scale = jnp.where(is_top, jnp.exp(jnp.minimum(stats - jnp.max(stats, axis=0, keepdims=True), 0.0)), 0.0)
    row_total = jnp.sum(scale * pltpu.roll(stats, HALF, 1), axis=0, keepdims=True)
    share = jnp.where(is_top, scale / jnp.where(is_top[0:1], row_total, 1.0), 0.0).T
    mixed = jnp.zeros((64, HD), F32)
    for k in range(chips):
        mixed = mixed + share[0:64, k : k + 1] * o_in[k, 0:64].astype(F32)
    row_f32[...] = mixed
    by_head = [row_f32[pl.ds(g, 8, stride=8), :] for g in range(GROUP)]
    d_all[core, chip] = jnp.concatenate(by_head, axis=0).astype(BF16)
    own_rows = d_all.at[core, chip]
    to_chips(6, lambda peer: own_rows, own_rows)
    wait_recv(6, d_all.at[0, pl.ds(0, chips - 1)])
    copy_to(d_all.at[core], d_all.at[core], 7, sibling, hd).start()

    pieces = m // 2

    def project(side_of):
        wide = d_all[side_of].astype(F32)
        wide = [wide[:, g * 8 : (g + 1) * 8, :].reshape(half_rows, HD) for g in range(GROUP)]
        wide = jnp.concatenate(wide, axis=1).astype(BF16)
        term = jnp.dot(wide, wo[...], preferred_element_type=F32).reshape(pieces, rows // m, wo.shape[1])
        e_f32[pl.ds(side_of * pieces, pieces)] = term
        e_out[pl.ds(side_of * pieces, pieces)] = term.astype(BF16)
        for j in range(pieces):
            to = side_of * pieces + lax.rem(hd + pieces // 2 + j, pieces)

            @pl.when(to != hd)
            def _():
                copy_to(e_out.at[to], e_in.at[lax.rem(hd - to - 1 + m, m)], 8, me, to).start()

    project(core)
    wait_recv(7, d_all.at[0])
    project(other)
    wait_recv(8, e_in)
    total = e_f32[hd]
    for k in range(m - 1):
        total = total + e_in[k].astype(F32)
    y_all[hd] = total.astype(BF16)

    for k in range(m - 1):
        copy_to(y_all.at[hd], y_all.at[hd], 9, me, head_at(k)).start()
    wait_recv(9, y_all.at[pl.ds(0, m - 1)])
    gathered = y_all[...].astype(F32).reshape(rows, wo.shape[1])
    for strip in range(wo.shape[1] // HD):
        cut = slice(strip * HD, (strip + 1) * HD)
        y_f32[strip] = gathered[:, cut]
        for c in range(2):
            for j in range(pair):
                for t in range(steps):
                    block = y_f32[strip, pl.ds(c * half_rows + j * steps + t, chips, stride=8), :]
                    y_rows[strip, pl.ds(t * requests + c * pair + j, chips, stride=2 * pair), :] = block
        out_ref[:, cut] = y_rows[strip].astype(BF16)

    wait_send(0, a_sib_in)
    wait_send(1, a_in.at[pl.ds(0, chips - 1)])
    wait_send(2, q_all.at[0, pl.ds(0, chips - 1)])
    wait_send(3, q_all.at[0])
    wait_send(4, o_in.at[pl.ds(0, chips - 1)])
    wait_send(5, o_sib_in)
    wait_send(6, d_all.at[0, pl.ds(0, chips - 1)])
    wait_send(7, d_all.at[0])
    wait_send(8, e_in)
    wait_send(9, y_all.at[pl.ds(0, m - 1)])


def solution(mesh):
    n, m = mesh.shape["seq"], mesh.shape["head"]

    def per_device(hidden_rows, norm_gain, w_query, key_up, key_factors, values, w_out, lengths, key_positions, query_start):
        steps, requests, features = hidden_rows.shape
        rows = steps * requests
        slots, rank = key_factors.shape[2], key_factors.shape[1]
        columns = w_out.shape[1]
        table = turn_tables()
        vmem, sem = pltpu.VMEM, pltpu.SemaphoreType.DMA
        hbm = pl.BlockSpec(memory_space=pl.ANY)
        y = pl.pallas_call(
            functools.partial(kernel, n, m, steps, requests, features * n),
            out_shape=pltpu.VMEM((rows, columns), BF16),
            in_specs=[hbm] * 11,
            out_specs=pl.BlockSpec(memory_space=vmem),
            scratch_shapes=[
                vmem((rows, features), BF16),
                vmem((features,), BF16),
                vmem(w_query.shape, BF16),
                vmem(key_up.shape, BF16),
                vmem((requests, rank, slots), BF16),
                vmem((requests, slots, HD), BF16),
                vmem(w_out.shape, BF16),
                vmem((requests, slots), jnp.int32),
                vmem(table.shape, F32),
                vmem((requests, HD, slots), BF16),
                vmem((n // 2, 2, 8, features), F32),
                vmem((n // 2, 2, 8, HD), F32),
                vmem((n // 2, 72, HD), F32),
                vmem((n // 2, 80, HD), BF16),
                vmem((n // 2, 80, HD), BF16),
                vmem((n // 2, 80, HD), BF16),
                vmem((n // 2, 80, HD), BF16),
                vmem((64, HD), F32),
                vmem((2, n // 2, 64, HD), BF16),
                vmem((n // 2, 80, HD), BF16),
                vmem((n // 2, 80, HD), BF16),
                vmem((n // 2, 80, HD), BF16),
                vmem((n // 2, 80, HD), BF16),
                vmem((2, n // 2, 64, HD), BF16),
                vmem((m, rows // m, columns), F32),
                vmem((m, rows // m, columns), BF16),
                vmem((m - 1, rows // m, columns), BF16),
                vmem((m, rows // m, columns), BF16),
                vmem((columns // HD, rows, HD), F32),
                vmem((columns // HD, rows, HD), F32),
                pltpu.SMEM((requests,), jnp.int32),
                pltpu.SMEM((requests,), jnp.int32),
                sem((9,)),
                sem((CHUNKS,)),
                sem((CHUNKS,)),
                sem((2,)),
                sem((10,)),
                sem((10,)),
            ],
            compiler_params=pltpu.CompilerParams(
                collective_id=0, has_side_effects=True, vmem_limit_bytes=56 * 2**20
            ),
            name="decode",
        )(
            hidden_rows.reshape(rows, features), norm_gain, w_query, key_up, key_factors,
            values, w_out, lengths, key_positions, query_start, jnp.asarray(table),
        )
        return y.reshape(steps, requests, columns)

    return jax.shard_map(
        per_device,
        mesh=mesh,
        in_specs=(
            P(None, None, "seq"),
            P("seq"),
            P("seq", "head"),
            P(None, "head"),
            P(None, None, "seq"),
            P(None, "seq", "head"),
            P("head", "seq"),
            P(),
            P(None, "seq"),
            P(),
        ),
        out_specs=P(None, None, "seq"),
        check_vma=False,
    )
```

```python
import functools
import math

import jax
import jax.numpy as jnp
import numpy as np
from jax import lax
from jax.experimental import pallas as pl
from jax.experimental.pallas import tpu as pltpu
from jax.sharding import PartitionSpec as P

HD = 128
HALF = 64
GROUP = 8
ROPE_BASE = 500000.0
NORM_EPSILON = 1e-05
DEAD = -1e30
MESH = pl.DeviceIdType.MESH
BF16 = jnp.bfloat16
F32 = jnp.float32
UNROLL = 4
KEY_CUTS = (0.0625, 0.5625)
CHUNKS = 4


def turn_tables():
    turns = ROPE_BASE ** (-2.0 * np.arange(HALF) / HD) / (2 * np.pi)
    mantissa, power = np.frexp(turns)
    head = np.ldexp(np.round(mantissa * 512) / 512, power)
    tail = turns - head
    rows = np.zeros((8, HD))
    rows[0], rows[1] = np.tile(head, 2), np.tile(tail, 2)
    columns = [np.broadcast_to(v[:, None], (HALF, HD)) for v in (head, tail)]
    return np.concatenate([*columns, rows]).astype(np.float32)


def chebyshev(function, terms):
    fit = np.polynomial.chebyshev.Chebyshev.interpolate(function, terms - 1, domain=[0, 0.25])
    return fit.convert(kind=np.polynomial.Polynomial).coef


COSINE = np.sqrt(2) * chebyshev(lambda z: np.cos(np.pi * np.sqrt(z)), 4)
SINE = np.sqrt(2) * chebyshev(lambda z: np.pi * np.sinc(np.sqrt(z)), 4)


def horner(coefficients, z):
    total = z * float(coefficients[-1]) + float(coefficients[-2])
    for c in coefficients[-3::-1]:
        total = total * z + float(c)
    return total


def cos_sin(position, head, tail):
    coarse, fine = position * head, position * tail
    part = (coarse - jnp.round(coarse + fine)) + fine
    square = part * part
    half_cosine, half_sine = horner(COSINE, square), part * horner(SINE, square)
    return 1.0 - half_sine * half_sine, half_sine * half_cosine


def far_first(side):
    def hops(d):
        return min(d, side - d)

    places = [(x, y) for x in range(side) for y in range(side)]
    places.sort(key=lambda p: -hops(p[0]) - hops(p[1]))
    return [x * side + y for x, y in places]


def kernel(
    n, m, steps, requests, width,
    hid_hbm, gain_hbm, wq_hbm, ku_hbm, fac_hbm, val_hbm, wo_hbm, len_hbm, pos_hbm, start_hbm, tab_hbm,
    out_ref,
    hid, gain, wq, ku, fac, val, wo, pos, tab, keys,
    scaled, square_f32, part, a_sib_out, a_sib_in, a_out, a_in, row_f32, q_all, o_sib_out, o_sib_in, o_out, o_in, d_all, e_f32, e_out, e_in, y_all,
    y_f32, y_rows, len_ref, start_ref, load_sem, fac_sem, val_sem, batch_sem, send_sem, recv_sem,
):
    me, hd = lax.axis_index("seq"), lax.axis_index("head")
    chip, core = me // 2, lax.rem(me, 2)
    other = 1 - core
    sibling = chip * 2 + other
    chips = n // 2
    side = math.isqrt(chips)
    slots = fac.shape[2]
    rows = steps * requests
    pair = requests // n
    per_step = requests // 8
    half_rows = rows // 2

    x, y = chip // side, lax.rem(chip, side)

    offsets = far_first(side)
    batch = chips // 4
    digits = [sum(offsets[i * batch + u] * 16**i for i in range(4)) for u in range(batch)]

    def chip_at(offset):
        over = lax.rem(x + lax.div(offset, side), side) * side
        return over + lax.rem(y + lax.rem(offset, side), side)

    near = [lax.rem(x + o // side, side) * side + lax.rem(y + o % side, side) for o in offsets]

    def batch_of(digits):
        return [chip_at(lax.rem(digit, 16)) for digit in digits]

    def after(digits):
        return [lax.div(digit, 16) for digit in digits]

    def head_at(k):
        away = (k + 1) // 2
        return lax.rem(hd + m + m // 2 + (-away if k % 2 else away), m)

    def copy_to(src, dst, phase, peer, head):
        return pltpu.make_async_remote_copy(
            src_ref=src, dst_ref=dst, send_sem=send_sem.at[phase], recv_sem=recv_sem.at[phase],
            device_id=(peer, head), device_id_type=MESH,
        )

    def to_chips(phase, src_of, dst):
        for k in range(chips - 1):
            peer = near[k]
            copy_to(src_of(peer), dst, phase, peer * 2 + core, hd).start()

    def wait_recv(phase, ref):
        copy_to(ref, ref, phase, sibling, hd).wait_recv()

    def wait_send(phase, ref):
        copy_to(ref, ref, phase, sibling, hd).wait_send()

    first = [(hid_hbm, hid), (gain_hbm, gain), (wq_hbm, wq), (tab_hbm, tab), (ku_hbm, ku), (pos_hbm, pos), (wo_hbm, wo)]
    first += [(len_hbm, len_ref), (start_hbm, start_ref)]
    loads = [pltpu.make_async_copy(src, dst, load_sem.at[i]) for i, (src, dst) in enumerate(first)]
    for copy in loads[:3]:
        copy.start()

    barrier = pltpu.get_barrier_semaphore()

    def greet(peer, head):
        pl.semaphore_signal(barrier, inc=1, device_id=(peer, head), device_id_type=MESH)

    for k in range(m - 1):
        greet(me, head_at(k))
    for k in range(chips - 1):
        greet(near[k] * 2 + core, hd)
    greet(sibling, hd)
    for copy in loads[3:]:
        copy.start()

    def big_load(src, dst, sem, i):
        block = pl.ds(i * (requests // CHUNKS), requests // CHUNKS)
        return pltpu.make_async_copy(src.at[block], dst.at[block], sem.at[i])

    key_steps = requests // UNROLL
    chunk_steps = key_steps // CHUNKS
    for i in range(CHUNKS):
        big_load(fac_hbm, fac, fac_sem, i).start()

    for copy in loads[:3]:
        copy.wait()
    widened = hid[...].astype(F32)
    squares = jnp.sum(widened * widened, axis=-1, keepdims=True)
    squares = jnp.broadcast_to(squares, (rows, HD)).reshape(chips, 2, 8, HD)
    scaled[...] = (widened * gain[...].astype(F32).reshape(1, -1)).reshape(scaled.shape)
    square_f32[...] = squares

    def terms(side_of):
        normed = scaled[:, side_of].reshape(half_rows, scaled.shape[3]).astype(BF16)
        found = []
        for g in range(0, GROUP, 2):
            term = jnp.dot(normed, wq[:, g * HD : (g + 2) * HD], preferred_element_type=F32)
            found += [term[:, 0:HD].reshape(chips, 8, HD), term[:, HD : 2 * HD].reshape(chips, 8, HD)]
        return jnp.concatenate([*found, square_f32[:, side_of]], axis=1)

    def packed(block):
        square = block[:, 64:72]
        head = square.astype(BF16).astype(F32)
        return jnp.concatenate([block[:, 0:64], head, square - head], axis=1).astype(BF16)

    def unpacked(block):
        block = block.astype(F32)
        return jnp.concatenate([block[..., 0:64, :], block[..., 64:72, :] + block[..., 72:80, :]], axis=-2)

    a_sib_out[...] = packed(terms(other))
    pl.semaphore_wait(barrier, chips + m - 1)
    copy_to(a_sib_out, a_sib_in, 0, sibling, hd).start()
    part[...] = terms(core)

    for copy in loads[3:]:
        copy.wait()
    step = me // per_step
    first_request = (me - step * per_step) * 8
    sublane = lax.broadcasted_iota(jnp.int32, (8, HD), 0)
    lane = lax.broadcasted_iota(jnp.int32, (8, HD), 1)
    where = jnp.zeros((8, HD), jnp.int32)
    for r in range(8):
        where = jnp.where(sublane == r, start_ref[first_request + r] + step, where)
    query_cosine, query_sine = cos_sin(where.astype(F32), tab[HD : HD + 1, :], tab[HD + 1 : HD + 2, :])
    query_sine = jnp.where(lane < HALF, -query_sine, query_sine)

    up_rows = ku[...].T

    def build_keys(i, _):
        @pl.when(lax.rem(i, chunk_steps) == 0)
        def _():
            big_load(fac_hbm, fac, fac_sem, i // chunk_steps).wait()

        for u in range(UNROLL):
            b = i * UNROLL + u
            raw = jnp.dot(up_rows, fac[b], preferred_element_type=F32)
            where = pos[pl.ds(b, 1), :].astype(F32)
            for block in range(slots // HD):
                cut = slice(block * HD, (block + 1) * HD)
                cosine, sine = cos_sin(where[:, cut], tab[0:HALF, :], tab[HALF : 2 * HALF, :])
                lower, upper = raw[0:HALF, cut], raw[HALF:HD, cut]
                keys[b, 0:HALF, cut] = (lower * cosine - upper * sine).astype(BF16)
                keys[b, HALF:HD, cut] = (upper * cosine + lower * sine).astype(BF16)
        return 0

    cuts = [round(key_steps * f) for f in KEY_CUTS]
    lax.fori_loop(0, cuts[0], build_keys, 0)
    wait_recv(0, a_sib_in)
    both_cores = part[...] + unpacked(a_sib_in[...])
    part[...] = both_cores
    a_out[...] = packed(both_cores)
    to_chips(1, lambda peer: a_out.at[peer], a_in.at[chip])
    for i in range(CHUNKS):
        big_load(val_hbm, val, val_sem, i).start()
    lax.fori_loop(cuts[0], cuts[1], build_keys, 0)

    wait_recv(1, a_in.at[pl.ds(0, chips - 1)])
    total = part[chip]
    for k in range(1, chips):
        total = total + unpacked(a_in[lax.rem(chip + k, chips)])
    mean_square = total[64:72] * (1.0 / width)
    projected = total[0:64].reshape(GROUP, 8, HD) * lax.rsqrt(mean_square + NORM_EPSILON)[None]
    flat = projected.reshape(64, HD)
    turned = pltpu.roll(flat, HALF, 1).reshape(GROUP, 8, HD)
    queries = (projected * query_cosine[None] + turned * query_sine[None]) * HD ** (-0.5)
    row_f32[...] = queries.reshape(64, HD)
    by_request = [row_f32[pl.ds(r, 8, stride=8), :] for r in range(8)]
    q_all[core, chip] = jnp.concatenate(by_request, axis=0).astype(BF16)
    mine = q_all.at[core, chip]
    to_chips(2, lambda peer: mine, mine)
    lax.fori_loop(cuts[1], key_steps, build_keys, 0)
    wait_recv(2, q_all.at[0, pl.ds(0, chips - 1)])
    copy_to(q_all.at[core], q_all.at[core], 3, sibling, hd).start()

    slot = lax.broadcasted_iota(jnp.int32, (1, slots), 1) + me * slots
    row64 = lax.broadcasted_iota(jnp.int32, (1, 64, HD), 1)
    lane64 = lax.broadcasted_iota(jnp.int32, (1, 64, HD), 2)
    row16 = lax.broadcasted_iota(jnp.int32, (1, 16, HD), 1)

    def queries_of(o):
        tile = o * pair // 8
        inside = pl.multiple_of((o * pair - tile * 8) * 8, 16)
        both = []
        for t in range(steps):
            from_rows = t * per_step + tile
            both.append(q_all[lax.rem(from_rows, 2), from_rows // 2, pl.ds(inside, 8 * pair), :].astype(F32))
        return [jnp.concatenate([x[8 * j : 8 * j + 8] for x in both], axis=0).astype(BF16) for j in range(pair)]

    def attend(owners):
        queries = [q for o in owners for q in queries_of(o)]
        requests_here = [o * pair + j for o in owners for j in range(pair)]
        scores = [jnp.dot(q, keys[b], preferred_element_type=F32) for q, b in zip(queries, requests_here)]
        live = [slot < len_ref[b] for b in requests_here]
        scores = [jnp.where(ok, x, DEAD) for ok, x in zip(live, scores)]
        tops = [jnp.max(x, axis=1, keepdims=True) for x in scores]
        exponents = [jnp.where(ok, jnp.exp(x - top), 0.0) for ok, x, top in zip(live, scores, tops)]
        totals = [jnp.sum(x, axis=1, keepdims=True) for x in exponents]
        mixes = [jnp.dot(x.astype(BF16), val[b], preferred_element_type=F32) for x, b in zip(exponents, requests_here)]
        return [jnp.concatenate(x, axis=0).reshape(len(owners), 64, -1) for x in (mixes, tops, totals)]

    def message(mix, top, total):
        stats = jnp.where(lane64 == row64, top, jnp.where(lane64 == row64 + HALF, total, 0.0))
        stats = jnp.sum(stats, axis=1, keepdims=True)
        high = stats.astype(BF16).astype(F32)
        middle = (stats - high).astype(BF16).astype(F32)
        low = stats - high - middle
        tail = jnp.where(row16 == 0, high, jnp.where(row16 == 1, middle, jnp.where(row16 == 2, low, 0.0)))
        return jnp.concatenate([mix, tail], axis=1).astype(BF16)

    def merged(mine, blocks):
        mix, top, total = mine
        blocks = blocks.astype(F32)
        stats = jnp.sum(blocks[:, 64:80], axis=1, keepdims=True)
        their_top = jnp.sum(jnp.where(lane64 == row64, stats, 0.0), axis=2, keepdims=True)
        their_total = jnp.sum(jnp.where(lane64 == row64 + HALF, stats, 0.0), axis=2, keepdims=True)
        both = jnp.maximum(top, their_top)
        ours, theirs = jnp.exp(top - both), jnp.exp(their_top - both)
        return mix * ours + blocks[:, 0:64] * theirs, both, total * ours + their_total * theirs

    for i in range(CHUNKS):
        big_load(val_hbm, val, val_sem, i).wait()
    def came_from(group):
        return [4 * (j // 2) + 2 * group + j % 2 for j in range(chips // 2)]

    def place_of(peer):
        return lax.rem(peer // 2, 2) * (chips // 2) + peer // 4 * 2 + lax.rem(peer, 2)

    def hand_over(i, src, dst, group):
        block = pl.ds(group * (chips // 2), chips // 2)
        return pltpu.make_async_remote_copy(
            src_ref=src.at[block], dst_ref=dst.at[block], send_sem=send_sem.at[5], recv_sem=batch_sem.at[i],
            device_id=(sibling, hd), device_id_type=MESH,
        )

    def for_sibling(i, _):
        @pl.when(i == 1)
        def _():
            wait_recv(3, q_all.at[0])

        group = lax.rem(core + i, 2)
        found = attend([peer * 2 + other for peer in came_from(group)])
        o_sib_out[pl.ds(group * (chips // 2), chips // 2)] = message(*found)
        hand_over(i, o_sib_out, o_sib_in, group).start()
        return 0

    def for_chips(i, digits):
        to = batch_of(digits)
        found = attend([peer * 2 + core for peer in to])

        @pl.when(i == 0)
        def _():
            for j in range(2):
                hand_over(j, o_sib_in, o_sib_in, lax.rem(other + j, 2)).wait_recv()

        theirs = jnp.stack([o_sib_in[place_of(peer)] for peer in to])
        blocks = message(*merged(found, theirs))
        for u, peer in enumerate(to):
            o_out[peer] = blocks[u]
        for peer in to[:-1]:
            copy_to(o_out.at[peer], o_in.at[chip], 4, peer * 2 + core, hd).start()

        @pl.when(i < 3)
        def _():
            copy_to(o_out.at[to[-1]], o_in.at[chip], 4, to[-1] * 2 + core, hd).start()

        return after(digits)

    lax.fori_loop(0, 2, for_sibling, 0)
    lax.fori_loop(0, 4, for_chips, [jnp.int32(digit) for digit in digits])
    o_in[chip] = o_out[chip]
    wait_recv(4, o_in.at[pl.ds(0, chips - 1)])
    stats = jnp.sum(o_in[:, 64:80, :].astype(F32), axis=1)
    is_top = lax.broadcasted_iota(jnp.int32, (chips, HD), 1) < HALF
    scale = jnp.where(is_top, jnp.exp(jnp.minimum(stats - jnp.max(stats, axis=0, keepdims=True), 0.0)), 0.0)
    row_total = jnp.sum(scale * pltpu.roll(stats, HALF, 1), axis=0, keepdims=True)
    share = jnp.where(is_top, scale / jnp.where(is_top[0:1], row_total, 1.0), 0.0).T
    mixed = jnp.zeros((64, HD), F32)
    for k in range(chips):
        mixed = mixed + share[0:64, k : k + 1] * o_in[k, 0:64].astype(F32)
    row_f32[...] = mixed
    by_head = [row_f32[pl.ds(g, 8, stride=8), :] for g in range(GROUP)]
    d_all[core, chip] = jnp.concatenate(by_head, axis=0).astype(BF16)
    own_rows = d_all.at[core, chip]
    to_chips(6, lambda peer: own_rows, own_rows)
    wait_recv(6, d_all.at[0, pl.ds(0, chips - 1)])
    copy_to(d_all.at[core], d_all.at[core], 7, sibling, hd).start()

    pieces = m // 2

    def project(side_of):
        wide = d_all[side_of].astype(F32)
        wide = [wide[:, g * 8 : (g + 1) * 8, :].reshape(half_rows, HD) for g in range(GROUP)]
        wide = jnp.concatenate(wide, axis=1).astype(BF16)
        term = jnp.dot(wide, wo[...], preferred_element_type=F32).reshape(pieces, rows // m, wo.shape[1])
        e_f32[pl.ds(side_of * pieces, pieces)] = term
        e_out[pl.ds(side_of * pieces, pieces)] = term.astype(BF16)
        for j in range(pieces):
            to = side_of * pieces + lax.rem(hd + pieces // 2 + j, pieces)

            @pl.when(to != hd)
            def _():
                copy_to(e_out.at[to], e_in.at[lax.rem(hd - to - 1 + m, m)], 8, me, to).start()

    project(core)
    wait_recv(7, d_all.at[0])
    project(other)
    wait_recv(8, e_in)
    total = e_f32[hd]
    for k in range(m - 1):
        total = total + e_in[k].astype(F32)
    y_all[hd] = total.astype(BF16)

    for k in range(m - 1):
        copy_to(y_all.at[hd], y_all.at[hd], 9, me, head_at(k)).start()
    wait_recv(9, y_all.at[pl.ds(0, m - 1)])
    gathered = y_all[...].astype(F32).reshape(rows, wo.shape[1])
    for strip in range(wo.shape[1] // HD):
        cut = slice(strip * HD, (strip + 1) * HD)
        y_f32[strip] = gathered[:, cut]
        for c in range(2):
            for j in range(pair):
                for t in range(steps):
                    block = y_f32[strip, pl.ds(c * half_rows + j * steps + t, chips, stride=8), :]
                    y_rows[strip, pl.ds(t * requests + c * pair + j, chips, stride=2 * pair), :] = block
        out_ref[:, cut] = y_rows[strip].astype(BF16)

    wait_send(0, a_sib_in)
    wait_send(1, a_in.at[pl.ds(0, chips - 1)])
    wait_send(2, q_all.at[0, pl.ds(0, chips - 1)])
    wait_send(3, q_all.at[0])
    wait_send(4, o_in.at[pl.ds(0, chips - 1)])
    wait_send(5, o_sib_in)
    wait_send(6, d_all.at[0, pl.ds(0, chips - 1)])
    wait_send(7, d_all.at[0])
    wait_send(8, e_in)
    wait_send(9, y_all.at[pl.ds(0, m - 1)])


def solution(mesh):
    n, m = mesh.shape["seq"], mesh.shape["head"]

    def per_device(hidden_rows, norm_gain, w_query, key_up, key_factors, values, w_out, lengths, key_positions, query_start):
        steps, requests, features = hidden_rows.shape
        rows = steps * requests
        slots, rank = key_factors.shape[2], key_factors.shape[1]
        columns = w_out.shape[1]
        table = turn_tables()
        vmem, sem = pltpu.VMEM, pltpu.SemaphoreType.DMA
        hbm = pl.BlockSpec(memory_space=pl.ANY)
        y = pl.pallas_call(
            functools.partial(kernel, n, m, steps, requests, features * n),
            out_shape=pltpu.VMEM((rows, columns), BF16),
            in_specs=[hbm] * 11,
            out_specs=pl.BlockSpec(memory_space=vmem),
            scratch_shapes=[
                vmem((rows, features), BF16),
                vmem((features,), BF16),
                vmem(w_query.shape, BF16),
                vmem(key_up.shape, BF16),
                vmem((requests, rank, slots), BF16),
                vmem((requests, slots, HD), BF16),
                vmem(w_out.shape, BF16),
                vmem((requests, slots), jnp.int32),
                vmem(table.shape, F32),
                vmem((requests, HD, slots), BF16),
                vmem((n // 2, 2, 8, features), F32),
                vmem((n // 2, 2, 8, HD), F32),
                vmem((n // 2, 72, HD), F32),
                vmem((n // 2, 80, HD), BF16),
                vmem((n // 2, 80, HD), BF16),
                vmem((n // 2, 80, HD), BF16),
                vmem((n // 2, 80, HD), BF16),
                vmem((64, HD), F32),
                vmem((2, n // 2, 64, HD), BF16),
                vmem((n // 2, 80, HD), BF16),
                vmem((n // 2, 80, HD), BF16),
                vmem((n // 2, 80, HD), BF16),
                vmem((n // 2, 80, HD), BF16),
                vmem((2, n // 2, 64, HD), BF16),
                vmem((m, rows // m, columns), F32),
                vmem((m, rows // m, columns), BF16),
                vmem((m - 1, rows // m, columns), BF16),
                vmem((m, rows // m, columns), BF16),
                vmem((columns // HD, rows, HD), F32),
                vmem((columns // HD, rows, HD), F32),
                pltpu.SMEM((requests,), jnp.int32),
                pltpu.SMEM((requests,), jnp.int32),
                sem((9,)),
                sem((CHUNKS,)),
                sem((CHUNKS,)),
                sem((2,)),
                sem((10,)),
                sem((10,)),
            ],
            compiler_params=pltpu.CompilerParams(
                collective_id=0, has_side_effects=True, vmem_limit_bytes=56 * 2**20
            ),
            name="decode",
        )(
            hidden_rows.reshape(rows, features), norm_gain, w_query, key_up, key_factors,
            values, w_out, lengths, key_positions, query_start, jnp.asarray(table),
        )
        return y.reshape(steps, requests, columns)

    return jax.shard_map(
        per_device,
        mesh=mesh,
        in_specs=(
            P(None, None, "seq"),
            P("seq"),
            P("seq", "head"),
            P(None, "head"),
            P(None, None, "seq"),
            P(None, "seq", "head"),
            P("head", "seq"),
            P(),
            P(None, "seq"),
            P(),
        ),
        out_specs=P(None, None, "seq"),
        check_vma=False,
    )
```

```python
import functools
import math

import jax
import jax.numpy as jnp
import numpy as np
from jax import lax
from jax.experimental import pallas as pl
from jax.experimental.pallas import tpu as pltpu
from jax.sharding import PartitionSpec as P

HD = 128
HALF = 64
GROUP = 8
ROPE_BASE = 500000.0
NORM_EPSILON = 1e-05
DEAD = -1e30
MESH = pl.DeviceIdType.MESH
BF16 = jnp.bfloat16
F32 = jnp.float32
UNROLL = 4
KEY_CUTS = (0.0625, 0.5625)
CHUNKS = 4


def turn_tables():
    turns = ROPE_BASE ** (-2.0 * np.arange(HALF) / HD) / (2 * np.pi)
    mantissa, power = np.frexp(turns)
    head = np.ldexp(np.round(mantissa * 512) / 512, power)
    tail = turns - head
    rows = np.zeros((8, HD))
    rows[0], rows[1] = np.tile(head, 2), np.tile(tail, 2)
    columns = [np.broadcast_to(v[:, None], (HALF, HD)) for v in (head, tail)]
    return np.concatenate([*columns, rows]).astype(np.float32)


def chebyshev(function, terms):
    fit = np.polynomial.chebyshev.Chebyshev.interpolate(function, terms - 1, domain=[0, 0.25])
    return fit.convert(kind=np.polynomial.Polynomial).coef


COSINE = np.sqrt(2) * chebyshev(lambda z: np.cos(np.pi * np.sqrt(z)), 4)
SINE = np.sqrt(2) * chebyshev(lambda z: np.pi * np.sinc(np.sqrt(z)), 4)


def horner(coefficients, z):
    total = z * float(coefficients[-1]) + float(coefficients[-2])
    for c in coefficients[-3::-1]:
        total = total * z + float(c)
    return total


def cos_sin(position, head, tail):
    coarse, fine = position * head, position * tail
    part = (coarse - jnp.round(coarse + fine)) + fine
    square = part * part
    half_cosine, half_sine = horner(COSINE, square), part * horner(SINE, square)
    return 1.0 - half_sine * half_sine, half_sine * half_cosine


def far_first(side):
    def hops(d):
        return min(d, side - d)

    places = [(x, y) for x in range(side) for y in range(side)]
    places.sort(key=lambda p: -hops(p[0]) - hops(p[1]))
    return [x * side + y for x, y in places]


def kernel(
    n, m, steps, requests, width,
    hid_hbm, gain_hbm, wq_hbm, ku_hbm, fac_hbm, val_hbm, wo_hbm, len_hbm, pos_hbm, start_hbm, tab_hbm,
    out_ref,
    hid, gain, wq, ku, fac, val, wo, pos, tab, keys,
    scaled, square_f32, part, a_sib_out, a_sib_in, a_out, a_in, row_f32, q_all, o_sib_out, o_sib_in, o_out, o_in, d_all, e_f32, e_out, e_in, y_all,
    y_f32, y_rows, len_ref, start_ref, load_sem, fac_sem, val_sem, batch_sem, send_sem, recv_sem,
):
    me, hd = lax.axis_index("seq"), lax.axis_index("head")
    chip, core = me // 2, lax.rem(me, 2)
    other = 1 - core
    sibling = chip * 2 + other
    chips = n // 2
    side = math.isqrt(chips)
    slots = fac.shape[2]
    rows = steps * requests
    pair = requests // n
    per_step = requests // 8
    half_rows = rows // 2

    x, y = chip // side, lax.rem(chip, side)

    offsets = far_first(side)
    batch = chips // 4
    near = [lax.rem(x + o // side, side) * side + lax.rem(y + o % side, side) for o in offsets]

    def head_at(k):
        away = (k + 1) // 2
        return lax.rem(hd + m + m // 2 + (-away if k % 2 else away), m)

    def copy_to(src, dst, phase, peer, head):
        return pltpu.make_async_remote_copy(
            src_ref=src, dst_ref=dst, send_sem=send_sem.at[phase], recv_sem=recv_sem.at[phase],
            device_id=(peer, head), device_id_type=MESH,
        )

    def to_chips(phase, src_of, dst):
        for k in range(chips - 1):
            peer = near[k]
            copy_to(src_of(peer), dst, phase, peer * 2 + core, hd).start()

    def wait_recv(phase, ref):
        copy_to(ref, ref, phase, sibling, hd).wait_recv()

    def wait_send(phase, ref):
        copy_to(ref, ref, phase, sibling, hd).wait_send()

    first = [(hid_hbm, hid), (gain_hbm, gain), (wq_hbm, wq), (tab_hbm, tab), (ku_hbm, ku), (pos_hbm, pos), (wo_hbm, wo)]
    first += [(len_hbm, len_ref), (start_hbm, start_ref)]
    loads = [pltpu.make_async_copy(src, dst, load_sem.at[i]) for i, (src, dst) in enumerate(first)]
    for copy in loads[:3]:
        copy.start()

    barrier = pltpu.get_barrier_semaphore()

    def greet(peer, head):
        pl.semaphore_signal(barrier, inc=1, device_id=(peer, head), device_id_type=MESH)

    for k in range(m - 1):
        greet(me, head_at(k))
    for k in range(chips - 1):
        greet(near[k] * 2 + core, hd)
    greet(sibling, hd)
    for copy in loads[3:]:
        copy.start()

    def big_load(src, dst, sem, i):
        block = pl.ds(i * (requests // CHUNKS), requests // CHUNKS)
        return pltpu.make_async_copy(src.at[block], dst.at[block], sem.at[i])

    key_steps = requests // UNROLL
    chunk_steps = key_steps // CHUNKS
    for i in range(CHUNKS):
        big_load(fac_hbm, fac, fac_sem, i).start()

    for copy in loads[:3]:
        copy.wait()
    widened = hid[...].astype(F32)
    squares = jnp.sum(widened * widened, axis=-1, keepdims=True)
    squares = jnp.broadcast_to(squares, (rows, HD)).reshape(chips, 2, 8, HD)
    scaled[...] = (widened * gain[...].astype(F32).reshape(1, -1)).reshape(scaled.shape)
    square_f32[...] = squares

    def terms(side_of):
        normed = scaled[:, side_of].reshape(half_rows, scaled.shape[3]).astype(BF16)
        found = []
        for g in range(0, GROUP, 2):
            term = jnp.dot(normed, wq[:, g * HD : (g + 2) * HD], preferred_element_type=F32)
            found += [term[:, 0:HD].reshape(chips, 8, HD), term[:, HD : 2 * HD].reshape(chips, 8, HD)]
        return jnp.concatenate([*found, square_f32[:, side_of]], axis=1)

    def packed(block):
        square = block[:, 64:72]
        head = square.astype(BF16).astype(F32)
        return jnp.concatenate([block[:, 0:64], head, square - head], axis=1).astype(BF16)

    def unpacked(block):
        block = block.astype(F32)
        return jnp.concatenate([block[..., 0:64, :], block[..., 64:72, :] + block[..., 72:80, :]], axis=-2)

    a_sib_out[...] = packed(terms(other))
    pl.semaphore_wait(barrier, chips + m - 1)
    copy_to(a_sib_out, a_sib_in, 0, sibling, hd).start()
    part[...] = terms(core)

    for copy in loads[3:]:
        copy.wait()
    step = me // per_step
    first_request = (me - step * per_step) * 8
    sublane = lax.broadcasted_iota(jnp.int32, (8, HD), 0)
    lane = lax.broadcasted_iota(jnp.int32, (8, HD), 1)
    where = jnp.zeros((8, HD), jnp.int32)
    for r in range(8):
        where = jnp.where(sublane == r, start_ref[first_request + r] + step, where)
    query_cosine, query_sine = cos_sin(where.astype(F32), tab[HD : HD + 1, :], tab[HD + 1 : HD + 2, :])
    query_sine = jnp.where(lane < HALF, -query_sine, query_sine)

    up_rows = ku[...].T

    def build_keys(i, _):
        @pl.when(lax.rem(i, chunk_steps) == 0)
        def _():
            big_load(fac_hbm, fac, fac_sem, i // chunk_steps).wait()

        for u in range(UNROLL):
            b = i * UNROLL + u
            raw = jnp.dot(up_rows, fac[b], preferred_element_type=F32)
            where = pos[pl.ds(b, 1), :].astype(F32)
            for block in range(slots // HD):
                cut = slice(block * HD, (block + 1) * HD)
                cosine, sine = cos_sin(where[:, cut], tab[0:HALF, :], tab[HALF : 2 * HALF, :])
                lower, upper = raw[0:HALF, cut], raw[HALF:HD, cut]
                keys[b, 0:HALF, cut] = (lower * cosine - upper * sine).astype(BF16)
                keys[b, HALF:HD, cut] = (upper * cosine + lower * sine).astype(BF16)
        return 0

    cuts = [round(key_steps * f) for f in KEY_CUTS]
    lax.fori_loop(0, cuts[0], build_keys, 0)
    wait_recv(0, a_sib_in)
    both_cores = part[...] + unpacked(a_sib_in[...])
    part[...] = both_cores
    a_out[...] = packed(both_cores)
    to_chips(1, lambda peer: a_out.at[peer], a_in.at[chip])
    for i in range(CHUNKS):
        big_load(val_hbm, val, val_sem, i).start()
    lax.fori_loop(cuts[0], cuts[1], build_keys, 0)

    wait_recv(1, a_in.at[pl.ds(0, chips - 1)])
    total = part[chip]
    for k in range(1, chips):
        total = total + unpacked(a_in[lax.rem(chip + k, chips)])
    mean_square = total[64:72] * (1.0 / width)
    projected = total[0:64].reshape(GROUP, 8, HD) * lax.rsqrt(mean_square + NORM_EPSILON)[None]
    flat = projected.reshape(64, HD)
    turned = pltpu.roll(flat, HALF, 1).reshape(GROUP, 8, HD)
    queries = (projected * query_cosine[None] + turned * query_sine[None]) * HD ** (-0.5)
    row_f32[...] = queries.reshape(64, HD)
    by_request = [row_f32[pl.ds(r, 8, stride=8), :] for r in range(8)]
    q_all[core, chip] = jnp.concatenate(by_request, axis=0).astype(BF16)
    mine = q_all.at[core, chip]
    to_chips(2, lambda peer: mine, mine)
    lax.fori_loop(cuts[1], key_steps, build_keys, 0)
    wait_recv(2, q_all.at[0, pl.ds(0, chips - 1)])
    copy_to(q_all.at[core], q_all.at[core], 3, sibling, hd).start()

    slot = lax.broadcasted_iota(jnp.int32, (1, slots), 1) + me * slots
    row64 = lax.broadcasted_iota(jnp.int32, (1, 64, HD), 1)
    lane64 = lax.broadcasted_iota(jnp.int32, (1, 64, HD), 2)
    row16 = lax.broadcasted_iota(jnp.int32, (1, 16, HD), 1)

    def queries_of(o):
        tile = o * pair // 8
        inside = pl.multiple_of((o * pair - tile * 8) * 8, 16)
        both = []
        for t in range(steps):
            from_rows = t * per_step + tile
            both.append(q_all[lax.rem(from_rows, 2), from_rows // 2, pl.ds(inside, 8 * pair), :].astype(F32))
        return [jnp.concatenate([x[8 * j : 8 * j + 8] for x in both], axis=0).astype(BF16) for j in range(pair)]

    def attend(owners):
        queries = [q for o in owners for q in queries_of(o)]
        requests_here = [o * pair + j for o in owners for j in range(pair)]
        scores = [jnp.dot(q, keys[b], preferred_element_type=F32) for q, b in zip(queries, requests_here)]
        live = [slot < len_ref[b] for b in requests_here]
        scores = [jnp.where(ok, x, DEAD) for ok, x in zip(live, scores)]
        tops = [jnp.max(x, axis=1, keepdims=True) for x in scores]
        exponents = [jnp.where(ok, jnp.exp(x - top), 0.0) for ok, x, top in zip(live, scores, tops)]
        totals = [jnp.sum(x, axis=1, keepdims=True) for x in exponents]
        mixes = [jnp.dot(x.astype(BF16), val[b], preferred_element_type=F32) for x, b in zip(exponents, requests_here)]
        return [jnp.concatenate(x, axis=0).reshape(len(owners), 64, -1) for x in (mixes, tops, totals)]

    def message(mix, top, total):
        stats = jnp.where(lane64 == row64, top, jnp.where(lane64 == row64 + HALF, total, 0.0))
        stats = jnp.sum(stats, axis=1, keepdims=True)
        high = stats.astype(BF16).astype(F32)
        middle = (stats - high).astype(BF16).astype(F32)
        low = stats - high - middle
        tail = jnp.where(row16 == 0, high, jnp.where(row16 == 1, middle, jnp.where(row16 == 2, low, 0.0)))
        return jnp.concatenate([mix, tail], axis=1).astype(BF16)

    def merged(mine, blocks):
        mix, top, total = mine
        blocks = blocks.astype(F32)
        stats = jnp.sum(blocks[:, 64:80], axis=1, keepdims=True)
        their_top = jnp.sum(jnp.where(lane64 == row64, stats, 0.0), axis=2, keepdims=True)
        their_total = jnp.sum(jnp.where(lane64 == row64 + HALF, stats, 0.0), axis=2, keepdims=True)
        both = jnp.maximum(top, their_top)
        ours, theirs = jnp.exp(top - both), jnp.exp(their_top - both)
        return mix * ours + blocks[:, 0:64] * theirs, both, total * ours + their_total * theirs

    for i in range(CHUNKS):
        big_load(val_hbm, val, val_sem, i).wait()
    def came_from(group):
        return [4 * (j // 2) + 2 * group + j % 2 for j in range(chips // 2)]

    def place_of(peer):
        return lax.rem(peer // 2, 2) * (chips // 2) + peer // 4 * 2 + lax.rem(peer, 2)

    def hand_over(i, src, dst, group):
        block = pl.ds(group * (chips // 2), chips // 2)
        return pltpu.make_async_remote_copy(
            src_ref=src.at[block], dst_ref=dst.at[block], send_sem=send_sem.at[5], recv_sem=batch_sem.at[i],
            device_id=(sibling, hd), device_id_type=MESH,
        )

    def for_sibling(i, _):
        @pl.when(i == 1)
        def _():
            wait_recv(3, q_all.at[0])

        group = lax.rem(core + i, 2)
        found = attend([peer * 2 + other for peer in came_from(group)])
        o_sib_out[pl.ds(group * (chips // 2), chips // 2)] = message(*found)
        hand_over(i, o_sib_out, o_sib_in, group).start()
        return 0

    def serve(to, is_first):
        found = attend([peer * 2 + core for peer in to])
        if is_first:
            for j in range(2):
                hand_over(j, o_sib_in, o_sib_in, lax.rem(other + j, 2)).wait_recv()
        theirs = jnp.stack([o_sib_in[place_of(peer)] for peer in to])
        blocks = message(*merged(found, theirs))
        for u, peer in enumerate(to):
            o_out[peer] = blocks[u]
        for peer in to:
            if peer is not near[-1]:
                copy_to(o_out.at[peer], o_in.at[chip], 4, peer * 2 + core, hd).start()

    lax.fori_loop(0, 2, for_sibling, 0)
    serve(near[: 2 * batch], True)
    serve(near[2 * batch : 3 * batch], False)
    serve(near[3 * batch :], False)
    o_in[chip] = o_out[chip]
    wait_recv(4, o_in.at[pl.ds(0, chips - 1)])
    stats = jnp.sum(o_in[:, 64:80, :].astype(F32), axis=1)
    is_top = lax.broadcasted_iota(jnp.int32, (chips, HD), 1) < HALF
    scale = jnp.where(is_top, jnp.exp(jnp.minimum(stats - jnp.max(stats, axis=0, keepdims=True), 0.0)), 0.0)
    row_total = jnp.sum(scale * pltpu.roll(stats, HALF, 1), axis=0, keepdims=True)
    share = jnp.where(is_top, scale / jnp.where(is_top[0:1], row_total, 1.0), 0.0).T
    mixed = jnp.zeros((64, HD), F32)
    for k in range(chips):
        mixed = mixed + share[0:64, k : k + 1] * o_in[k, 0:64].astype(F32)
    row_f32[...] = mixed
    by_head = [row_f32[pl.ds(g, 8, stride=8), :] for g in range(GROUP)]
    d_all[core, chip] = jnp.concatenate(by_head, axis=0).astype(BF16)
    own_rows = d_all.at[core, chip]
    to_chips(6, lambda peer: own_rows, own_rows)
    wait_recv(6, d_all.at[0, pl.ds(0, chips - 1)])
    copy_to(d_all.at[core], d_all.at[core], 7, sibling, hd).start()

    pieces = m // 2

    def project(side_of):
        wide = d_all[side_of].astype(F32)
        wide = [wide[:, g * 8 : (g + 1) * 8, :].reshape(half_rows, HD) for g in range(GROUP)]
        wide = jnp.concatenate(wide, axis=1).astype(BF16)
        term = jnp.dot(wide, wo[...], preferred_element_type=F32).reshape(pieces, rows // m, wo.shape[1])
        e_f32[pl.ds(side_of * pieces, pieces)] = term
        e_out[pl.ds(side_of * pieces, pieces)] = term.astype(BF16)
        for j in range(pieces):
            to = side_of * pieces + lax.rem(hd + pieces // 2 + j, pieces)

            @pl.when(to != hd)
            def _():
                copy_to(e_out.at[to], e_in.at[lax.rem(hd - to - 1 + m, m)], 8, me, to).start()

    project(core)
    wait_recv(7, d_all.at[0])
    project(other)
    wait_recv(8, e_in)
    total = e_f32[hd]
    for k in range(m - 1):
        total = total + e_in[k].astype(F32)
    y_all[hd] = total.astype(BF16)

    for k in range(m - 1):
        copy_to(y_all.at[hd], y_all.at[hd], 9, me, head_at(k)).start()
    wait_recv(9, y_all.at[pl.ds(0, m - 1)])
    gathered = y_all[...].astype(F32).reshape(rows, wo.shape[1])
    for strip in range(wo.shape[1] // HD):
        cut = slice(strip * HD, (strip + 1) * HD)
        y_f32[strip] = gathered[:, cut]
        for c in range(2):
            for j in range(pair):
                for t in range(steps):
                    block = y_f32[strip, pl.ds(c * half_rows + j * steps + t, chips, stride=8), :]
                    y_rows[strip, pl.ds(t * requests + c * pair + j, chips, stride=2 * pair), :] = block
        out_ref[:, cut] = y_rows[strip].astype(BF16)

    wait_send(0, a_sib_in)
    wait_send(1, a_in.at[pl.ds(0, chips - 1)])
    wait_send(2, q_all.at[0, pl.ds(0, chips - 1)])
    wait_send(3, q_all.at[0])
    wait_send(4, o_in.at[pl.ds(0, chips - 1)])
    wait_send(5, o_sib_in)
    wait_send(6, d_all.at[0, pl.ds(0, chips - 1)])
    wait_send(7, d_all.at[0])
    wait_send(8, e_in)
    wait_send(9, y_all.at[pl.ds(0, m - 1)])


def solution(mesh):
    n, m = mesh.shape["seq"], mesh.shape["head"]

    def per_device(hidden_rows, norm_gain, w_query, key_up, key_factors, values, w_out, lengths, key_positions, query_start):
        steps, requests, features = hidden_rows.shape
        rows = steps * requests
        slots, rank = key_factors.shape[2], key_factors.shape[1]
        columns = w_out.shape[1]
        table = turn_tables()
        vmem, sem = pltpu.VMEM, pltpu.SemaphoreType.DMA
        hbm = pl.BlockSpec(memory_space=pl.ANY)
        y = pl.pallas_call(
            functools.partial(kernel, n, m, steps, requests, features * n),
            out_shape=pltpu.VMEM((rows, columns), BF16),
            in_specs=[hbm] * 11,
            out_specs=pl.BlockSpec(memory_space=vmem),
            scratch_shapes=[
                vmem((rows, features), BF16),
                vmem((features,), BF16),
                vmem(w_query.shape, BF16),
                vmem(key_up.shape, BF16),
                vmem((requests, rank, slots), BF16),
                vmem((requests, slots, HD), BF16),
                vmem(w_out.shape, BF16),
                vmem((requests, slots), jnp.int32),
                vmem(table.shape, F32),
                vmem((requests, HD, slots), BF16),
                vmem((n // 2, 2, 8, features), F32),
                vmem((n // 2, 2, 8, HD), F32),
                vmem((n // 2, 72, HD), F32),
                vmem((n // 2, 80, HD), BF16),
                vmem((n // 2, 80, HD), BF16),
                vmem((n // 2, 80, HD), BF16),
                vmem((n // 2, 80, HD), BF16),
                vmem((64, HD), F32),
                vmem((2, n // 2, 64, HD), BF16),
                vmem((n // 2, 80, HD), BF16),
                vmem((n // 2, 80, HD), BF16),
                vmem((n // 2, 80, HD), BF16),
                vmem((n // 2, 80, HD), BF16),
                vmem((2, n // 2, 64, HD), BF16),
                vmem((m, rows // m, columns), F32),
                vmem((m, rows // m, columns), BF16),
                vmem((m - 1, rows // m, columns), BF16),
                vmem((m, rows // m, columns), BF16),
                vmem((columns // HD, rows, HD), F32),
                vmem((columns // HD, rows, HD), F32),
                pltpu.SMEM((requests,), jnp.int32),
                pltpu.SMEM((requests,), jnp.int32),
                sem((9,)),
                sem((CHUNKS,)),
                sem((CHUNKS,)),
                sem((2,)),
                sem((10,)),
                sem((10,)),
            ],
            compiler_params=pltpu.CompilerParams(
                collective_id=0, has_side_effects=True, vmem_limit_bytes=56 * 2**20
            ),
            name="decode",
        )(
            hidden_rows.reshape(rows, features), norm_gain, w_query, key_up, key_factors,
            values, w_out, lengths, key_positions, query_start, jnp.asarray(table),
        )
        return y.reshape(steps, requests, columns)

    return jax.shard_map(
        per_device,
        mesh=mesh,
        in_specs=(
            P(None, None, "seq"),
            P("seq"),
            P("seq", "head"),
            P(None, "head"),
            P(None, None, "seq"),
            P(None, "seq", "head"),
            P("head", "seq"),
            P(),
            P(None, "seq"),
            P(),
        ),
        out_specs=P(None, None, "seq"),
        check_vma=False,
    )
```
